128 devices in a mesh: dap: 64 (over z_hi, y, x, core), dp: 2 (over z_lo).
Axes of the slice: x: 4, y: 4, z: 4 (z_hi: 2, z_lo: 2; z = z_hi * 2 + z_lo), core: 2. Of those that a mesh axis runs over, the one named last changes fastest.
Arguments:
- pair: bfloat16 [1536, 768, 128], P(('dp', 'dap')), parts along dimension 0, may hold values from -6 to 6
- pair_mask: int32 [1536, 768], P('dp', 'dap'), parts along dimension 0, may hold values 0 or 1
- ln_gain: float32 [128], replicated, may hold values from 0.1 to 1.9
- ln_offset: float32 [128], replicated, may hold values from -3 to 3
- bias_weight: bfloat16 [128, 4], replicated, may hold values from -14.142136 to 14.142136
- query_weight: bfloat16 [128, 128], replicated, may hold values from -2.4748737 to 2.4748737
- key_weight: bfloat16 [128, 128], replicated, may hold values from -2.4748737 to 2.4748737
- value_weight: bfloat16 [128, 128], replicated, may hold values from -0.5 to 0.5
- gate_weight: bfloat16 [128, 128], replicated, may hold values from -0.5 to 0.5
- gate_offset: float32 [128], replicated, may hold values from -4 to 4
- out_weight: bfloat16 [128, 128], replicated, may hold values from -0.5 to 0.5
- out_offset: float32 [128], replicated, may hold values from -3 to 3
Outputs:
- update: bfloat16 [1536, 768, 128], P(('dp', 'dap')), parts along dimension 0
The draws below stay inside these ranges and needn't reach their ends.
There are 2 independent parts, one for each index of `dp`. The reference program is written for one: setup_inputs(seed, part) draws one part's arguments, and reference() takes and returns one part's arrays. A program takes and returns all parts, laid end to end along the dimension named above; an argument that names none is the same for every part. Nothing has to cross between parts.
All inputs are finite; a program needn't handle non-finite values. No bound on the sum of `pair_mask` on one device may be relied on, other than what follows from the above.
Results may differ from the reference program's by a relative error of at most 0.014.
The reference program's roundings to bfloat16 on the way (of `normed`, `bias`, `gate`, `probs_low` and `gated`) count: a program that leaves them out, or rounds other values in their place, can miss the bound.
Values may be sent and summed in bfloat16 or wider, within the bound.
No kernel may reach another device: no remote copies, remote signals or barrier semaphores. Data moves between devices by JAX's collectives and lax.ppermute only.
A program may use at most 128 MiB of HBM per device.

```python
import jax
import jax.numpy as jnp
from jax import lax

CHANNELS = 128
HEADS = 4
HEAD_DIM = 32
RESIDUES = 768


def clipped_matrix(key, rows, cols):
    base = jnp.clip(jax.random.normal(key, (rows, cols), jnp.float32), -4.0, 4.0)
    return (base / CHANNELS ** 0.5).astype(jnp.bfloat16)


def draw_bias_weight(key, part):
    key = jax.random.fold_in(key, 11)
    return clipped_matrix(key, CHANNELS, HEADS)


def draw_query_weight(key, part):
    key = jax.random.fold_in(key, 23)
    return clipped_matrix(key, CHANNELS, CHANNELS)


def draw_key_weight(key, part):
    key = jax.random.fold_in(key, 37)
    return clipped_matrix(key, CHANNELS, CHANNELS)


def plant(result, own_key, least, top_value):
    place = [jax.random.randint(jax.random.fold_in(own_key, axis), (), 0, length) for axis, length in enumerate(result.shape)]
    widest = result.shape.index(max(result.shape))
    next_to = place[:widest] + [(place[widest] + 1) % result.shape[widest]] + place[widest + 1:]
    return result.at[tuple(place)].set(least).at[tuple(next_to)].set(top_value)


def levels(rng, dims, split, low, largest):
    level, own = 1.0, jax.random.fold_in(rng, 6)
    for axis_at, blocks in split:
        heights = jnp.exp(jax.random.uniform(jax.random.fold_in(own, axis_at), (blocks,), jnp.float32, low / len(split), largest / len(split)))
        level = level * jnp.repeat(heights, dims[axis_at] // blocks).reshape([-1 if axis == axis_at else 1 for axis in range(len(dims))])
    return level


def bell_draw(own_key, dims, scale, most, split=(), held_as=jnp.bfloat16):
    result = scale * jax.random.normal(own_key, dims, jnp.float32)
    if split:
        result = result * levels(own_key, dims, split, -0.22, 0.18)
    return jnp.clip(result, -most, most).astype(held_as)


def setup_inputs(seed: int = 0, part: int = 0) -> dict:
    splits = jax.random.split(jax.random.key(seed), 13)
    own_keys = jax.random.split(jax.random.fold_in(splits[12], part), 13)
    pair = bell_draw(own_keys[0], (RESIDUES, RESIDUES, CHANNELS), 1.0, 6.0, ((0, 64),))
    pair_mask = plant((jax.random.randint(own_keys[1], (RESIDUES, RESIDUES), 0, 8) < 7).astype(jnp.int32), jax.random.fold_in(own_keys[1], 1), 0, 1)
    ln_gain = jnp.clip(1.0 + 0.18 * jax.random.normal(splits[2], (CHANNELS,), jnp.float32), 0.1, 1.9)
    ln_offset = bell_draw(splits[3], (CHANNELS,), 0.3, 3.0, (), jnp.float32)
    bias_weight = draw_bias_weight(jax.random.fold_in(splits[12], 71), part)
    query_weight = draw_query_weight(jax.random.fold_in(splits[12], 71), part)
    key_weight = draw_key_weight(jax.random.fold_in(splits[12], 71), part)
    value_weight = bell_draw(splits[7], (CHANNELS, CHANNELS), CHANNELS ** -0.5, 0.5)
    gate_weight = bell_draw(splits[8], (CHANNELS, CHANNELS), CHANNELS ** -0.5, 0.5)
    gate_offset = bell_draw(splits[9], (CHANNELS,), 1.0, 4.0, (), jnp.float32)
    out_weight = bell_draw(splits[10], (CHANNELS, CHANNELS), CHANNELS ** -0.5, 0.5)
    out_offset = bell_draw(splits[11], (CHANNELS,), 0.3, 3.0, (), jnp.float32)
    return {"pair": pair, "pair_mask": pair_mask, "ln_gain": ln_gain, "ln_offset": ln_offset, "bias_weight": bias_weight, "query_weight": query_weight, "key_weight": key_weight, "value_weight": value_weight, "gate_weight": gate_weight, "gate_offset": gate_offset, "out_weight": out_weight, "out_offset": out_offset}


NEG_BIG = 1000000000.0
EPSILON = 1e-05

def layer_norm(values_in, ln_gain, ln_offset):
    wide = values_in.astype(jnp.float32)
    centre = lax.optimization_barrier(jnp.mean(wide, axis=-1, keepdims=True))
    spread = lax.optimization_barrier(jnp.mean((wide - centre) ** 2, axis=-1, keepdims=True))
    return (wide - centre) * lax.rsqrt(spread + EPSILON) * ln_gain + ln_offset

def reference(pair, pair_mask, ln_gain, ln_offset, bias_weight, query_weight, key_weight, value_weight, gate_weight, gate_offset, out_weight, out_offset):
    normed = layer_norm(pair, ln_gain, ln_offset).astype(jnp.bfloat16)
    flat_rows = normed.reshape(RESIDUES * RESIDUES, CHANNELS)
    bias = jnp.dot(flat_rows, bias_weight, preferred_element_type=jnp.float32).astype(jnp.bfloat16)
    bias = jnp.transpose(bias.reshape(RESIDUES, RESIDUES, HEADS), (2, 0, 1))
    query = (jnp.dot(flat_rows, query_weight, preferred_element_type=jnp.float32) * HEAD_DIM ** (-0.5)).astype(jnp.bfloat16)
    keys_all = jnp.dot(flat_rows, key_weight, preferred_element_type=jnp.float32).astype(jnp.bfloat16)
    values_all = jnp.dot(flat_rows, value_weight, preferred_element_type=jnp.float32).astype(jnp.bfloat16)
    gate = jax.nn.sigmoid(jnp.dot(flat_rows, gate_weight, preferred_element_type=jnp.float32) + gate_offset).astype(jnp.bfloat16)
    shape_heads = (RESIDUES, RESIDUES, HEADS, HEAD_DIM)
    query_cols = jnp.swapaxes(query.reshape(shape_heads), 0, 1)
    key_cols = jnp.swapaxes(keys_all.reshape(shape_heads), 0, 1)
    value_cols = jnp.swapaxes(values_all.reshape(shape_heads), 0, 1)
    mask_cols = jnp.transpose(pair_mask)
    bias_wide = bias.astype(jnp.float32)

    def per_column(column_args):
        query_one, key_one, value_one, mask_one = column_args
        scores = jnp.einsum('ihd,khd->hki', query_one.astype(jnp.float32), key_one.astype(jnp.float32), precision=lax.Precision.HIGHEST)
        scores = scores + bias_wide + NEG_BIG * (mask_one.astype(jnp.float32) - 1.0)[None, :, None]
        top = lax.optimization_barrier(jnp.max(scores, axis=1, keepdims=True))
        probs = jnp.exp(scores - top)
        totals = lax.optimization_barrier(jnp.sum(probs, axis=1))
        probs_low = probs.astype(jnp.bfloat16).astype(jnp.float32)
        weighted = jnp.einsum('hki,khd->hid', probs_low, value_one.astype(jnp.float32), precision=lax.Precision.HIGHEST)
        return jnp.transpose(weighted / totals[..., None], (1, 0, 2))
    attended = lax.map(per_column, (query_cols, key_cols, value_cols, mask_cols))
    attended = jnp.swapaxes(attended, 0, 1).reshape(RESIDUES * RESIDUES, CHANNELS)
    gated = (attended * gate.astype(jnp.float32)).astype(jnp.bfloat16)
    update = jnp.dot(gated, out_weight, preferred_element_type=jnp.float32) + out_offset
    return update.astype(jnp.bfloat16).reshape(RESIDUES, RESIDUES, CHANNELS)
```

```python
import functools

import jax
import jax.numpy as jnp
from jax import lax
from jax.experimental import pallas as pl
from jax.experimental.pallas import tpu as pltpu
from jax.sharding import PartitionSpec as P

NEG_BIG = 1000000000.0
EPSILON = 1e-05
CHUNKS = 2
TOTAL_LOW = 1e-20
TOTAL_HIGH = 1e30
NT = (((1,), (1,)), ((), ()))


def dot(lhs, rhs):
    return jnp.dot(lhs, rhs, preferred_element_type=jnp.float32)


def dot_nt(lhs, rhs):
    return lax.dot_general(lhs, rhs, NT, preferred_element_type=jnp.float32)


def in_vmem(count):
    return [pl.BlockSpec(memory_space=pltpu.VMEM)] * count


def prepare_kernel(rows, width, groups, chunks, heads, pair_ref, gain_ref, offset_ref, bias_weight_ref, *refs):
    chunk_refs, bias_ref = refs[:chunks], refs[chunks]
    normed_ref, bias_wide_ref = refs[chunks + 1], refs[chunks + 2]
    staged_refs = refs[chunks + 3 :]
    cols = width // groups
    per = cols // chunks
    channels = pair_ref.shape[1]
    average = jnp.full((2 * channels, channels), 1.0 / channels, jnp.bfloat16)
    weight = bias_weight_ref[...].astype(jnp.float32).T.astype(jnp.bfloat16)
    for row in range(rows):
        block = pair_ref[pl.ds(row * width, width), :]
        wide = block.astype(jnp.float32)
        centred = wide - dot(block, average[:channels])
        square = centred * centred
        high = square.astype(jnp.bfloat16)
        low = (square - high.astype(jnp.float32)).astype(jnp.bfloat16)
        spread = dot(jnp.concatenate([high, low], axis=1), average)
        normed = (centred * lax.rsqrt(spread + EPSILON) * gain_ref[...] + offset_ref[...]).astype(jnp.bfloat16)
        normed_ref[pl.ds(row * width, width), :] = normed.astype(jnp.float32)
        bias_wide_ref[pl.ds(row * heads, heads), :] = dot_nt(weight, normed)
        for col in range(cols):
            chunk, place = divmod(col, per)
            staged_refs[chunk][pl.ds(row * per + place, groups, stride=rows * per), :] = normed_ref[
                pl.ds(row * width + col, groups, stride=cols), :
            ]
    for chunk in range(chunks):
        chunk_refs[chunk][...] = staged_refs[chunk][...].astype(jnp.bfloat16)
    bias_ref[...] = bias_wide_ref[...].astype(jnp.bfloat16)


def turn_kernel(heads, gathered_ref, turned_ref, wide_ref):
    width = gathered_ref.shape[1]
    tile = wide_ref.shape[2]
    for at in range(0, width, tile):
        wide_ref[at // tile] = gathered_ref[:, at : at + tile].astype(jnp.float32)
    unit = (
        lax.broadcasted_iota(jnp.int32, (tile, tile), 0) == lax.broadcasted_iota(jnp.int32, (tile, tile), 1)
    ).astype(jnp.bfloat16)
    for head in range(heads):
        for at in range(0, width, tile):
            one = wide_ref[at // tile, pl.ds(head, width, stride=heads), :].astype(jnp.bfloat16)
            turned_ref[head, pl.ds(at, tile), :] = dot_nt(unit, one).astype(jnp.bfloat16)


def attend_kernel(
    chunk,
    per,
    heads,
    moved_ref,
    bias_ref,
    mask_ref,
    query_weight_ref,
    key_weight_ref,
    value_weight_ref,
    gate_weight_ref,
    gate_offset_ref,
    out_ref,
    source_ref,
    weight_ref,
    key_ref,
    value_ref,
    result_ref,
    fine_ref,
):
    channels = moved_ref.shape[1]
    width = mask_ref.shape[0]
    mask_cols = mask_ref.shape[1]
    head_dim = channels // heads
    source_ref[...] = moved_ref[...].astype(jnp.float32)
    for at, ref in enumerate((query_weight_ref, key_weight_ref, value_weight_ref, gate_weight_ref)):
        weight_ref[:, at * channels : (at + 1) * channels] = ref[...]
    lane_head = lax.broadcasted_iota(jnp.int32, (1, channels), 1) // head_dim
    own = [(lane_head == head).astype(jnp.bfloat16) for head in range(heads)]
    fine_ref[...] = jnp.ones_like(fine_ref)

    def project(col):
        source = source_ref[pl.ds(col, width, stride=per), :].astype(jnp.bfloat16)
        wide = dot(source, weight_ref[...])
        query = (wide[:, :channels] * head_dim ** (-0.5)).astype(jnp.bfloat16)
        keys = wide[:, channels : 2 * channels].astype(jnp.bfloat16)
        values = wide[:, 2 * channels : 3 * channels].astype(jnp.bfloat16)
        gate = jax.nn.sigmoid(wide[:, 3 * channels :] + gate_offset_ref[...]).astype(jnp.bfloat16)
        pick = (lax.broadcasted_iota(jnp.int32, (mask_cols, channels), 0) == chunk * per + col).astype(jnp.bfloat16)
        present = dot(mask_ref[...].astype(jnp.float32).astype(jnp.bfloat16), pick).astype(jnp.bfloat16)
        for head in range(heads):
            key_ref[head] = keys * own[head]
        return query, values, gate.astype(jnp.float32), present

    def column(col, carry):
        query, values, gate, present = project(col)
        shown = values * present
        for head in range(heads):
            value_ref[head, :, :channels] = shown * own[head]
            value_ref[head, :, channels:] = present * own[head]
        total = jnp.zeros((width, 2 * channels), jnp.float32)
        for head in range(heads):
            scores = dot_nt(query, key_ref[head]) + bias_ref[head].astype(jnp.float32)
            total += dot(jnp.exp(scores).astype(jnp.bfloat16), value_ref[head])
        sums = total[:, channels:]
        fine = jnp.where((sums > TOTAL_LOW) & (sums < TOTAL_HIGH), 1.0, 0.0)
        fine_ref[...] = jnp.minimum(fine_ref[...], jnp.min(fine.reshape(width // 8, 8, channels), axis=0))
        result_ref[pl.ds(col, width, stride=per), :] = total[:, :channels] / sums * gate
        return carry

    lax.fori_loop(0, per, column, 0)

    @pl.when(jnp.min(fine_ref[...]) < 0.5)
    def _():
        tile = 128

        def exact(col, carry):
            query, values, gate, present = project(col)
            first = (lax.broadcasted_iota(jnp.int32, (8, channels), 1) == 0).astype(jnp.bfloat16)
            lift = NEG_BIG * (dot_nt(first, present)[:1] - 1.0)
            for head in range(heads):
                value_ref[head, :, :channels] = values * own[head]
            parts = []
            for at in range(0, width, tile):
                attended = jnp.zeros((tile, channels), jnp.float32)
                for head in range(heads):
                    scores = dot_nt(query[at : at + tile], key_ref[head])
                    scores = scores + bias_ref[head, at : at + tile, :].astype(jnp.float32) + lift
                    probs = jnp.exp(scores - jnp.max(scores, axis=1, keepdims=True))
                    totals = jnp.sum(probs, axis=1, keepdims=True)
                    attended += dot(probs.astype(jnp.bfloat16), value_ref[head, :, :channels]) / totals
                parts.append(attended)
            result_ref[pl.ds(col, width, stride=per), :] = jnp.concatenate(parts, axis=0) * gate
            return carry

        lax.fori_loop(0, per, exact, 0)

    out_ref[...] = result_ref[...].astype(jnp.bfloat16)


def finish_kernel(rows, width, groups, chunks, *refs):
    chunk_refs = refs[:chunks]
    out_weight_ref, out_offset_ref, update_ref = refs[chunks : chunks + 3]
    wide_refs = refs[chunks + 3 : 2 * chunks + 3]
    row_ref = refs[2 * chunks + 3]
    cols = width // groups
    per = cols // chunks
    for chunk in range(chunks):
        wide_refs[chunk][...] = dot(chunk_refs[chunk][...], out_weight_ref[...]) + out_offset_ref[...]
    for row in range(rows):
        for col in range(cols):
            chunk, place = divmod(col, per)
            row_ref[row % 2, pl.ds(col, groups, stride=cols), :] = wide_refs[chunk][
                pl.ds(row * per + place, groups, stride=rows * per), :
            ]
        update_ref[pl.ds(row * width, width), :] = row_ref[row % 2].astype(jnp.bfloat16)


def local(
    pair,
    pair_mask,
    ln_gain,
    ln_offset,
    bias_weight,
    query_weight,
    key_weight,
    value_weight,
    gate_weight,
    gate_offset,
    out_weight,
    out_offset,
):
    rows, width, channels = pair.shape
    groups = lax.axis_size("dap")
    cols = width // groups
    per = cols // CHUNKS
    heads = bias_weight.shape[1]
    block = groups * rows * per
    low, wide = jnp.bfloat16, jnp.float32
    params = pltpu.CompilerParams(vmem_limit_bytes=56 * 1024 * 1024)
    *sends, bias_local = pl.pallas_call(
        functools.partial(prepare_kernel, rows, width, groups, CHUNKS, heads),
        out_shape=[jax.ShapeDtypeStruct((block, channels), low)] * CHUNKS
        + [jax.ShapeDtypeStruct((rows * heads, width), low)],
        in_specs=in_vmem(4),
        out_specs=in_vmem(CHUNKS + 1),
        scratch_shapes=[pltpu.VMEM((rows * width, channels), wide), pltpu.VMEM((rows * heads, width), wide)]
        + [pltpu.VMEM((block, channels), wide)] * CHUNKS,
        compiler_params=params,
        name="prepare",
    )(pair.reshape(rows * width, channels), ln_gain.reshape(1, channels), ln_offset.reshape(1, channels), bias_weight)

    gathered = lax.all_gather(bias_local, "dap", axis=0, tiled=True)
    moved = [
        lax.all_to_all(
            send.reshape(groups, rows * per, channels), "dap", split_axis=0, concat_axis=0, tiled=True
        ).reshape(block, channels)
        for send in sends
    ]
    turned = pl.pallas_call(
        functools.partial(turn_kernel, heads),
        out_shape=jax.ShapeDtypeStruct((heads, width, width), low),
        in_specs=in_vmem(1),
        out_specs=in_vmem(1)[0],
        scratch_shapes=[pltpu.VMEM((width // channels, width * heads, channels), wide)],
        compiler_params=params,
        name="turn",
    )(gathered)

    returned = []
    for chunk in range(CHUNKS):
        gated = pl.pallas_call(
            functools.partial(attend_kernel, chunk, per, heads),
            out_shape=jax.ShapeDtypeStruct((block, channels), low),
            in_specs=in_vmem(8),
            out_specs=in_vmem(1)[0],
            scratch_shapes=[
                pltpu.VMEM((block, channels), wide),
                pltpu.VMEM((channels, 4 * channels), low),
                pltpu.VMEM((heads, width, channels), low),
                pltpu.VMEM((heads, width, 2 * channels), low),
                pltpu.VMEM((block, channels), wide),
                pltpu.VMEM((8, channels), wide),
            ],
            compiler_params=params,
            cost_estimate=pl.CostEstimate(
                flops=per * heads * width * width * channels * 6,
                bytes_accessed=2 * heads * width * width,
                transcendentals=per * heads * width * width,
            ),
            name="attend",
        )(
            moved[chunk],
            turned,
            pair_mask,
            query_weight,
            key_weight,
            value_weight,
            gate_weight,
            gate_offset.reshape(1, channels),
        )
        returned.append(
            lax.all_to_all(
                gated.reshape(groups, rows * per, channels), "dap", split_axis=0, concat_axis=0, tiled=True
            ).reshape(block, channels)
        )
    update = pl.pallas_call(
        functools.partial(finish_kernel, rows, width, groups, CHUNKS),
        out_shape=jax.ShapeDtypeStruct((rows * width, channels), low),
        in_specs=in_vmem(CHUNKS + 2),
        out_specs=in_vmem(1)[0],
        scratch_shapes=[pltpu.VMEM((block, channels), wide)] * CHUNKS + [pltpu.VMEM((2, width, channels), wide)],
        compiler_params=params,
        name="finish",
    )(*returned, out_weight, out_offset.reshape(1, channels))
    return update.reshape(rows, width, channels)


def solution(mesh):
    in_specs = (P(("dp", "dap"), None, None), P("dp", "dap")) + (P(),) * 10
    out_specs = P(("dp", "dap"), None, None)
    return jax.shard_map(local, mesh=mesh, in_specs=in_specs, out_specs=out_specs, check_vma=False)
```

```python
import functools

import jax
import jax.numpy as jnp
from jax import lax
from jax.experimental import pallas as pl
from jax.experimental.pallas import tpu as pltpu
from jax.sharding import PartitionSpec as P

NEG_BIG = 1000000000.0
EPSILON = 1e-05
CHUNKS = 2
TOTAL_LOW = 1e-20
TOTAL_HIGH = 1e30
NT = (((1,), (1,)), ((), ()))
PLACE = ("z", "y", "x", "core")
PLACE_SIZES = (2, 4, 4, 2)
TOTAL = 64
FIRST = 8
SHIFTS = (0, 1, 2, 3)


def dot(lhs, rhs):
    return jnp.dot(lhs, rhs, preferred_element_type=jnp.float32)


def dot_nt(lhs, rhs):
    return lax.dot_general(lhs, rhs, NT, preferred_element_type=jnp.float32)


def in_vmem(count):
    return [pl.BlockSpec(memory_space=pltpu.VMEM)] * count


def norm_kernel(rows, width, heads, pair_ref, gain_ref, offset_ref, bias_weight_ref, normed_ref, bias_ref, wide_ref):
    weight = bias_weight_ref[...]
    blank = jnp.zeros_like(weight)
    both = jnp.concatenate(
        [jnp.concatenate([weight, blank], axis=1), jnp.concatenate([blank, weight], axis=1)], axis=0
    )
    for row in range(rows):
        wide = pair_ref[pl.ds(row * width, width), :].astype(jnp.float32)
        centred = wide - jnp.mean(wide, axis=1, keepdims=True)
        spread = jnp.mean(centred * centred, axis=1, keepdims=True)
        normed = centred * lax.rsqrt(spread + EPSILON) * gain_ref[...] + offset_ref[...]
        normed_ref[pl.ds(row * width, width), :] = normed.astype(jnp.bfloat16)
        if row % 2:
            two = [normed_ref[pl.ds(at * width, width), :] for at in (row - 1, row)]
            wide_ref[pl.ds((row - 1) * heads, 2 * heads), :] = dot_nt(both, jnp.concatenate(two, axis=1))
    for copy in range(bias_ref.shape[0] // (rows * heads)):
        bias_ref[pl.ds(copy * rows * heads, rows * heads), :] = wide_ref[...].astype(jnp.bfloat16)


def layout_kernel(rows, width, groups, chunks, normed_ref, *refs):
    chunk_refs, wide_ref, staged_refs = refs[:chunks], refs[chunks], refs[chunks + 1 :]
    cols = width // groups
    per = cols // chunks
    for row in range(rows):
        wide_ref[row % 2] = normed_ref[pl.ds(row * width, width), :].astype(jnp.float32)
        for col in range(cols):
            chunk, place = divmod(col, per)
            staged_refs[chunk][pl.ds(row * per + place, groups, stride=rows * per), :] = wide_ref[
                row % 2, pl.ds(col, groups, stride=cols), :
            ]
    for chunk in range(chunks):
        chunk_refs[chunk][...] = staged_refs[chunk][...].astype(jnp.bfloat16)


def hold_kernel(*refs):
    pass


def hold(*arrays):
    whole = [pl.BlockSpec(memory_space=pl.ANY)] * len(arrays)
    return pl.pallas_call(
        hold_kernel,
        out_shape=[jax.ShapeDtypeStruct(one.shape, one.dtype) for one in arrays],
        in_specs=whole,
        out_specs=whole,
        input_output_aliases={at: at for at in range(len(arrays))},
        name="hold",
    )(*arrays)


def place_of(index):
    place = {}
    for axis, size in zip(reversed(PLACE), reversed(PLACE_SIZES)):
        place[axis] = index % size if isinstance(index, int) else lax.rem(index, size)
        index = index // size
    return place


def index_of(place):
    index = 0
    for axis, size in zip(PLACE, PLACE_SIZES):
        index = index * size + place[axis]
    return index


ORDER = (("y", "x"), ("x", "y"))


def first_groups():
    groups = {}
    for index in range(TOTAL):
        place = place_of(index)
        groups.setdefault((place["core"], place[ORDER[place["core"]][1]]), []).append(index)
    return list(groups.values())


def second_pairs(step):
    pairs = []
    for index in range(TOTAL):
        place = place_of(index)
        axis = ORDER[place["core"]][1]
        pairs.append((index, index_of({**place, axis: (place[axis] + step) % 4})))
    return pairs


def gather_bias(bias_copies, sends):
    first = lax.all_to_all(
        bias_copies.reshape((FIRST, bias_copies.shape[0] // FIRST, bias_copies.shape[1])),
        "dap",
        split_axis=0,
        concat_axis=0,
        axis_index_groups=first_groups(),
        tiled=True,
    ).reshape(bias_copies.shape)
    first, *sends = hold(first, *sends)
    pieces = [first if step == 0 else lax.ppermute(first, "dap", second_pairs(step)) for step in SHIFTS]
    other_core = [(index, index ^ 1) for index in range(TOTAL)]
    return pieces + [lax.ppermute(piece, "dap", other_core) for piece in pieces], sends


def turn_kernel(heads, rows, handed, *refs):
    count = 2 * len(SHIFTS)
    pieces, turned_ref, wide_ref = refs[:count], refs[count + handed], refs[-1]
    width = turned_ref.shape[1]
    tile = wide_ref.shape[2]
    here = place_of(lax.axis_index("dap"))
    block = rows * heads

    def unpack(core, my_pieces):
        first, second = ORDER[core]
        for far, step in enumerate(SHIFTS):
            for place in range(FIRST):
                at = {
                    "z": place // 4,
                    "core": core,
                    first: place % 4,
                    second: lax.rem(here[second] + 4 - step, 4),
                }
                start = pl.multiple_of(index_of(at) * block, 16)
                for lane in range(width // tile):
                    wide_ref[lane, pl.ds(start, block), :] = my_pieces[far][
                        pl.ds(place * block, block), lane * tile : (lane + 1) * tile
                    ].astype(jnp.float32)

    for core in range(2):

        @pl.when(here["core"] == core)
        def _():
            unpack(core, pieces[: len(SHIFTS)])
            unpack(1 - core, pieces[len(SHIFTS) :])

    unit = (
        lax.broadcasted_iota(jnp.int32, (tile, tile), 0) == lax.broadcasted_iota(jnp.int32, (tile, tile), 1)
    ).astype(jnp.bfloat16)
    for head in range(heads):
        for at in range(0, width, tile):
            one = wide_ref[at // tile, pl.ds(head, width, stride=heads), :].astype(jnp.bfloat16)
            turned_ref[head, pl.ds(at, tile), :] = dot_nt(unit, one).astype(jnp.bfloat16)


def attend_kernel(
    chunk,
    per,
    heads,
    moved_ref,
    bias_ref,
    mask_ref,
    query_weight_ref,
    key_weight_ref,
    value_weight_ref,
    gate_weight_ref,
    gate_offset_ref,
    out_ref,
    source_ref,
    weight_ref,
    present_ref,
    result_ref,
    fine_ref,
    *sets,
):
    channels = moved_ref.shape[1]
    width, mask_cols = mask_ref.shape
    head_dim = channels // heads
    source_ref[...] = moved_ref[...].astype(jnp.float32)
    for at, ref in enumerate((query_weight_ref, key_weight_ref, value_weight_ref, gate_weight_ref)):
        weight_ref[:, at * channels : (at + 1) * channels] = ref[...]
    present_ref[...] = mask_ref[...].astype(jnp.float32).astype(jnp.bfloat16)
    lane_head = lax.broadcasted_iota(jnp.int32, (1, channels), 1) // head_dim
    own = [(lane_head == head).astype(jnp.bfloat16) for head in range(heads)]
    fine_ref[...] = jnp.ones_like(fine_ref)
    share = width // heads
    first_set, second_set = sets[:5], sets[5:]

    def project(col, part, buffers, hide=True):
        query_ref, key_ref, value_ref, gate_ref, _ = buffers
        rows = pl.ds(part * share, share)
        source = source_ref[pl.ds(col + part * share * per, share, stride=per), :].astype(jnp.bfloat16)
        wide = dot(source, weight_ref[...])
        query_ref[rows, :] = (wide[:, :channels] * head_dim ** (-0.5)).astype(jnp.bfloat16)
        key_ref[rows, :] = wide[:, channels : 2 * channels].astype(jnp.bfloat16)
        pick = (lax.broadcasted_iota(jnp.int32, (mask_cols, channels), 0) == chunk * per + col).astype(jnp.bfloat16)
        present = dot(present_ref[rows, :], pick).astype(jnp.bfloat16)
        values = wide[:, 2 * channels : 3 * channels].astype(jnp.bfloat16)
        value_ref[rows, :channels] = values * present if hide else values
        value_ref[rows, channels:] = present
        gate_ref[rows, :] = jax.nn.sigmoid(wide[:, 3 * channels :] + gate_offset_ref[...]).astype(jnp.bfloat16)

    def attend(head, buffers):
        query_ref, key_ref, value_ref, _, total_ref = buffers
        scores = dot_nt(query_ref[...] * own[head], key_ref[...]) + bias_ref[head].astype(jnp.float32)
        total = dot(jnp.exp(scores).astype(jnp.bfloat16), value_ref[...])
        for low in (head * head_dim, channels + head * head_dim):
            total_ref[:, low : low + head_dim] = total[:, low : low + head_dim]

    def close(col, buffers):
        _, _, _, gate_ref, total_ref = buffers
        sums = total_ref[:, channels:]
        fine = jnp.where((sums > TOTAL_LOW) & (sums < TOTAL_HIGH), 1.0, 0.0)
        fine_ref[...] = jnp.minimum(fine_ref[...], jnp.min(fine.reshape(width // 8, 8, channels), axis=0))
        result_ref[pl.ds(col, width, stride=per), :] = (
            total_ref[:, :channels] / sums * gate_ref[...].astype(jnp.float32)
        )

    for part in range(heads):
        project(0, part, first_set)

    def two_columns(step, carry):
        for now, later, col in ((first_set, second_set, 2 * step), (second_set, first_set, 2 * step + 1)):
            for head in range(heads):
                attend(head, now)
                project(jnp.minimum(col + 1, per - 1), head, later)
            close(col, now)
        return carry

    lax.fori_loop(0, per // 2, two_columns, 0)

    @pl.when(jnp.min(fine_ref[...]) < 0.5)
    def _():
        tile = 128
        query_ref, key_ref, value_ref, gate_ref, total_ref = first_set

        def exact(col, carry):
            for part in range(heads):
                project(col, part, first_set, hide=False)
            first = (lax.broadcasted_iota(jnp.int32, (8, channels), 1) == 0).astype(jnp.bfloat16)
            lift = NEG_BIG * (dot_nt(first, value_ref[:, channels:])[:1] - 1.0)

            def rows_exact(step, inner):
                rows = pl.ds(pl.multiple_of(step * tile, tile), tile)
                for head in range(heads):
                    low = head * head_dim
                    scores = dot_nt(query_ref[rows, :] * own[head], key_ref[...])
                    scores = scores + bias_ref[head, rows, :].astype(jnp.float32) + lift
                    probs = jnp.exp(scores - jnp.max(scores, axis=1, keepdims=True))
                    totals = jnp.sum(probs, axis=1, keepdims=True)
                    attended = dot(probs.astype(jnp.bfloat16), value_ref[:, :channels]) / totals
                    total_ref[rows, low : low + head_dim] = attended[:, low : low + head_dim]
                return inner

            lax.fori_loop(0, width // tile, rows_exact, 0)
            result_ref[pl.ds(col, width, stride=per), :] = total_ref[:, :channels] * gate_ref[...].astype(jnp.float32)
            return carry

        lax.fori_loop(0, per, exact, 0)

    out_ref[...] = result_ref[...].astype(jnp.bfloat16)


def finish_kernel(rows, width, groups, chunks, *refs):
    chunk_refs = refs[:chunks]
    out_weight_ref, out_offset_ref, update_ref = refs[chunks : chunks + 3]
    wide_refs = refs[chunks + 3 : 2 * chunks + 3]
    row_ref = refs[2 * chunks + 3]
    cols = width // groups
    per = cols // chunks
    for chunk in range(chunks):
        wide_refs[chunk][...] = dot(chunk_refs[chunk][...], out_weight_ref[...]) + out_offset_ref[...]
    for row in range(rows):
        for col in range(cols):
            chunk, place = divmod(col, per)
            row_ref[row % 2, pl.ds(col, groups, stride=cols), :] = wide_refs[chunk][
                pl.ds(row * per + place, groups, stride=rows * per), :
            ]
        update_ref[pl.ds(row * width, width), :] = row_ref[row % 2].astype(jnp.bfloat16)


def local(
    pair,
    pair_mask,
    ln_gain,
    ln_offset,
    bias_weight,
    query_weight,
    key_weight,
    value_weight,
    gate_weight,
    gate_offset,
    out_weight,
    out_offset,
):
    rows, width, channels = pair.shape
    groups = lax.axis_size("dap")
    cols = width // groups
    per = cols // CHUNKS
    heads = bias_weight.shape[1]
    block = groups * rows * per
    low, wide = jnp.bfloat16, jnp.float32
    params = pltpu.CompilerParams(vmem_limit_bytes=56 * 1024 * 1024)
    normed, bias_copies = pl.pallas_call(
        functools.partial(norm_kernel, rows, width, heads),
        out_shape=[
            jax.ShapeDtypeStruct((rows * width, channels), low),
            jax.ShapeDtypeStruct((FIRST * rows * heads, width), low),
        ],
        in_specs=in_vmem(4),
        out_specs=in_vmem(2),
        scratch_shapes=[pltpu.VMEM((rows * heads, width), wide)],
        compiler_params=params,
        name="norm",
    )(pair.reshape(rows * width, channels), ln_gain.reshape(1, channels), ln_offset.reshape(1, channels), bias_weight.T)
    sends = pl.pallas_call(
        functools.partial(layout_kernel, rows, width, groups, CHUNKS),
        out_shape=[jax.ShapeDtypeStruct((block, channels), low)] * CHUNKS,
        in_specs=in_vmem(1),
        out_specs=in_vmem(CHUNKS),
        scratch_shapes=[pltpu.VMEM((2, width, channels), wide)] + [pltpu.VMEM((block, channels), wide)] * CHUNKS,
        compiler_params=params,
        cost_estimate=pl.CostEstimate(flops=10**6, bytes_accessed=15 * 10**6, transcendentals=0),
        name="layout",
    )(normed)

    pieces, sends = gather_bias(bias_copies, sends)
    whole = pl.BlockSpec(memory_space=pl.ANY)
    later = sends[1:]
    turned, *later = pl.pallas_call(
        functools.partial(turn_kernel, heads, rows, len(later)),
        out_shape=[jax.ShapeDtypeStruct((heads, width, width), low)]
        + [jax.ShapeDtypeStruct(one.shape, one.dtype) for one in later],
        in_specs=in_vmem(len(pieces)) + [whole] * len(later),
        out_specs=in_vmem(1) + [whole] * len(later),
        input_output_aliases={len(pieces) + at: 1 + at for at in range(len(later))},
        scratch_shapes=[pltpu.VMEM((width // channels, width * heads, channels), wide)],
        compiler_params=params,
        name="turn",
    )(*pieces, *later)
    moved = [
        lax.all_to_all(
            send.reshape(groups, rows * per, channels), "dap", split_axis=0, concat_axis=0, tiled=True
        ).reshape(block, channels)
        for send in (sends[0], *later)
    ]

    returned = []
    for chunk in range(CHUNKS):
        gated = pl.pallas_call(
            functools.partial(attend_kernel, chunk, per, heads),
            out_shape=jax.ShapeDtypeStruct((block, channels), low),
            in_specs=in_vmem(8),
            out_specs=in_vmem(1)[0],
            scratch_shapes=[
                pltpu.VMEM((block, channels), wide),
                pltpu.VMEM((channels, 4 * channels), low),
                pltpu.VMEM(pair_mask.shape, low),
                pltpu.VMEM((block, channels), wide),
                pltpu.VMEM((8, channels), wide),
            ]
            + 2
            * [
                pltpu.VMEM((width, channels), low),
                pltpu.VMEM((width, channels), low),
                pltpu.VMEM((width, 2 * channels), low),
                pltpu.VMEM((width, channels), low),
                pltpu.VMEM((width, 2 * channels), wide),
            ],
            compiler_params=params,
            cost_estimate=pl.CostEstimate(
                flops=per * heads * width * width * channels * 6,
                bytes_accessed=2 * heads * width * width,
                transcendentals=per * heads * width * width,
            ),
            name="attend",
        )(
            moved[chunk],
            turned,
            pair_mask,
            query_weight,
            key_weight,
            value_weight,
            gate_weight,
            gate_offset.reshape(1, channels),
        )
        returned.append(
            lax.all_to_all(
                gated.reshape(groups, rows * per, channels), "dap", split_axis=0, concat_axis=0, tiled=True
            ).reshape(block, channels)
        )
    update = pl.pallas_call(
        functools.partial(finish_kernel, rows, width, groups, CHUNKS),
        out_shape=jax.ShapeDtypeStruct((rows * width, channels), low),
        in_specs=in_vmem(CHUNKS + 2),
        out_specs=in_vmem(1)[0],
        scratch_shapes=[pltpu.VMEM((block, channels), wide)] * CHUNKS + [pltpu.VMEM((2, width, channels), wide)],
        compiler_params=params,
        name="finish",
    )(*returned, out_weight, out_offset.reshape(1, channels))
    return update.reshape(rows, width, channels)


def solution(mesh):
    in_specs = (P(("dp", "dap"), None, None), P("dp", "dap")) + (P(),) * 10
    out_specs = P(("dp", "dap"), None, None)
    return jax.shard_map(local, mesh=mesh, in_specs=in_specs, out_specs=out_specs, check_vma=False)
```

```python
import functools

import jax
import jax.numpy as jnp
from jax import lax
from jax.experimental import pallas as pl
from jax.experimental.pallas import tpu as pltpu
from jax.sharding import PartitionSpec as P

NEG_BIG = 1000000000.0
EPSILON = 1e-05
CHUNKS = 2
ATTEND_MIB = 40
TURN_MIB = 60
TOTAL_LOW = 1e-20
TOTAL_HIGH = 1e30
NT = (((1,), (1,)), ((), ()))
PLACE = ("z", "y", "x", "core")
PLACE_SIZES = (2, 4, 4, 2)
TOTAL = 64
FIRST = 8
SHIFTS = (0, 1, 2, 3)


def dot(lhs, rhs):
    return jnp.dot(lhs, rhs, preferred_element_type=jnp.float32)


def dot_nt(lhs, rhs):
    return lax.dot_general(lhs, rhs, NT, preferred_element_type=jnp.float32)


def in_vmem(count):
    return [pl.BlockSpec(memory_space=pltpu.VMEM)] * count


def norm_kernel(rows, width, heads, pair_ref, gain_ref, offset_ref, bias_weight_ref, normed_ref, bias_ref, wide_ref):
    weight = bias_weight_ref[...]
    blank = jnp.zeros_like(weight)
    both = jnp.concatenate(
        [jnp.concatenate([weight, blank], axis=1), jnp.concatenate([blank, weight], axis=1)], axis=0
    )
    for row in range(rows):
        wide = pair_ref[pl.ds(row * width, width), :].astype(jnp.float32)
        centred = wide - jnp.mean(wide, axis=1, keepdims=True)
        spread = jnp.mean(centred * centred, axis=1, keepdims=True)
        normed = centred * lax.rsqrt(spread + EPSILON) * gain_ref[...] + offset_ref[...]
        normed_ref[pl.ds(row * width, width), :] = normed.astype(jnp.bfloat16)
        if row % 2:
            two = [normed_ref[pl.ds(at * width, width), :] for at in (row - 1, row)]
            wide_ref[pl.ds((row - 1) * heads, 2 * heads), :] = dot_nt(both, jnp.concatenate(two, axis=1))
    for copy in range(bias_ref.shape[0] // (rows * heads)):
        bias_ref[pl.ds(copy * rows * heads, rows * heads), :] = wide_ref[...].astype(jnp.bfloat16)


def layout_kernel(rows, width, groups, chunks, normed_ref, mask_ref, *refs):
    weight_refs, chunk_refs = refs[:4], refs[4 : 4 + chunks]
    present_ref, packed_ref, wide_ref = refs[4 + chunks : 7 + chunks]
    staged_refs = refs[7 + chunks :]
    cols = width // groups
    per = cols // chunks
    for row in range(rows):
        wide_ref[row % 2] = normed_ref[pl.ds(row * width, width), :].astype(jnp.float32)
        for col in range(cols):
            chunk, place = divmod(col, per)
            staged_refs[chunk][pl.ds(row * per + place, groups, stride=rows * per), :] = wide_ref[
                row % 2, pl.ds(col, groups, stride=cols), :
            ]
    for chunk in range(chunks):
        chunk_refs[chunk][...] = staged_refs[chunk][...].astype(jnp.bfloat16)
    present_ref[...] = mask_ref[...].astype(jnp.float32).T.astype(jnp.bfloat16)
    channels = normed_ref.shape[1]
    for at, ref in enumerate(weight_refs):
        packed_ref[:, at * channels : (at + 1) * channels] = ref[...]


def hold_kernel(*refs):
    pass


def hold(*arrays):
    whole = [pl.BlockSpec(memory_space=pl.ANY)] * len(arrays)
    return pl.pallas_call(
        hold_kernel,
        out_shape=[jax.ShapeDtypeStruct(one.shape, one.dtype) for one in arrays],
        in_specs=whole,
        out_specs=whole,
        input_output_aliases={at: at for at in range(len(arrays))},
        name="hold",
    )(*arrays)


def place_of(index):
    place = {}
    for axis, size in zip(reversed(PLACE), reversed(PLACE_SIZES)):
        place[axis] = index % size if isinstance(index, int) else lax.rem(index, size)
        index = index // size
    return place


def index_of(place):
    index = 0
    for axis, size in zip(PLACE, PLACE_SIZES):
        index = index * size + place[axis]
    return index


ORDER = (("y", "x"), ("x", "y"))


def first_groups():
    groups = {}
    for index in range(TOTAL):
        place = place_of(index)
        groups.setdefault((place["core"], place[ORDER[place["core"]][1]]), []).append(index)
    return list(groups.values())


def second_pairs(step):
    pairs = []
    for index in range(TOTAL):
        place = place_of(index)
        axis = ORDER[place["core"]][1]
        pairs.append((index, index_of({**place, axis: (place[axis] + step) % 4})))
    return pairs


def gather_bias(bias_copies, sends):
    first = lax.all_to_all(
        bias_copies.reshape((FIRST, bias_copies.shape[0] // FIRST, bias_copies.shape[1])),
        "dap",
        split_axis=0,
        concat_axis=0,
        axis_index_groups=first_groups(),
        tiled=True,
    ).reshape(bias_copies.shape)
    first, *sends = hold(first, *sends)
    pieces = [first if step == 0 else lax.ppermute(first, "dap", second_pairs(step)) for step in SHIFTS]
    other_core = [(index, index ^ 1) for index in range(TOTAL)]
    return pieces + [lax.ppermute(piece, "dap", other_core) for piece in pieces], sends


def turn_kernel(heads, rows, handed, *refs):
    count = 2 * len(SHIFTS)
    pieces, turned_ref, wide_ref = refs[:count], refs[count + handed], refs[-1]
    width = turned_ref.shape[1]
    tile = wide_ref.shape[2]
    here = place_of(lax.axis_index("dap"))
    block = rows * heads

    def unpack(core, my_pieces):
        first, second = ORDER[core]
        for far, step in enumerate(SHIFTS):
            for place in range(FIRST):
                at = {
                    "z": place // 4,
                    "core": core,
                    first: place % 4,
                    second: lax.rem(here[second] + 4 - step, 4),
                }
                start = pl.multiple_of(index_of(at) * block, 16)
                for lane in range(width // tile):
                    wide_ref[lane, pl.ds(start, block), :] = my_pieces[far][
                        pl.ds(place * block, block), lane * tile : (lane + 1) * tile
                    ].astype(jnp.float32)

    for core in range(2):

        @pl.when(here["core"] == core)
        def _():
            unpack(core, pieces[: len(SHIFTS)])
            unpack(1 - core, pieces[len(SHIFTS) :])

    unit = (
        lax.broadcasted_iota(jnp.int32, (tile, tile), 0) == lax.broadcasted_iota(jnp.int32, (tile, tile), 1)
    ).astype(jnp.bfloat16)
    for head in range(heads):
        for at in range(0, width, tile):
            one = wide_ref[at // tile, pl.ds(head, width, stride=heads), :].astype(jnp.bfloat16)
            turned_ref[head, pl.ds(at, tile), :] = dot_nt(unit, one).astype(jnp.bfloat16)


def attend_kernel(
    chunk,
    per,
    heads,
    moved_ref,
    bias_ref,
    present_ref,
    weight_ref,
    gate_offset_ref,
    out_ref,
    source_ref,
    result_ref,
    fine_ref,
    *sets,
):
    channels = moved_ref.shape[1]
    width, mask_cols = present_ref.shape
    head_dim = channels // heads
    source_ref[...] = moved_ref[...].astype(jnp.float32)
    lane_head = lax.broadcasted_iota(jnp.int32, (1, channels), 1) // head_dim
    own = [(lane_head == head).astype(jnp.bfloat16) for head in range(heads)]
    fine_ref[...] = jnp.ones_like(fine_ref)
    share = width // heads
    first_set, second_set = sets[:5], sets[5:]

    def project(col, part, buffers, hide=True):
        query_ref, key_ref, value_ref, gate_ref, _ = buffers
        rows = pl.ds(part * share, share)
        source = source_ref[pl.ds(col + part * share * per, share, stride=per), :].astype(jnp.bfloat16)
        wide = dot(source, weight_ref[...])
        query_ref[rows, :] = (wide[:, :channels] * head_dim ** (-0.5)).astype(jnp.bfloat16)
        key_ref[rows, :] = wide[:, channels : 2 * channels].astype(jnp.bfloat16)
        pick = (lax.broadcasted_iota(jnp.int32, (mask_cols, channels), 0) == chunk * per + col).astype(jnp.bfloat16)
        present = dot(present_ref[rows, :], pick).astype(jnp.bfloat16)
        values = wide[:, 2 * channels : 3 * channels].astype(jnp.bfloat16)
        value_ref[rows, :channels] = values * present if hide else values
        value_ref[rows, channels:] = present
        gate_ref[rows, :] = jax.nn.sigmoid(wide[:, 3 * channels :] + gate_offset_ref[...]).astype(jnp.bfloat16)

    def attend(head, buffers):
        query_ref, key_ref, value_ref, _, total_ref = buffers
        scores = dot_nt(query_ref[...] * own[head], key_ref[...]) + bias_ref[head].astype(jnp.float32)
        total = dot(jnp.exp(scores).astype(jnp.bfloat16), value_ref[...])
        for low in (head * head_dim, channels + head * head_dim):
            total_ref[:, low : low + head_dim] = total[:, low : low + head_dim]

    def close(col, buffers):
        _, _, _, gate_ref, total_ref = buffers
        sums = total_ref[:, channels:]
        fine = jnp.where((sums > TOTAL_LOW) & (sums < TOTAL_HIGH), 1.0, 0.0)
        fine_ref[...] = jnp.minimum(fine_ref[...], jnp.min(fine.reshape(width // 8, 8, channels), axis=0))
        result_ref[pl.ds(col, width, stride=per), :] = (
            total_ref[:, :channels] / sums * gate_ref[...].astype(jnp.float32)
        )

    for part in range(heads):
        project(0, part, first_set)

    def column(col, now, later=None):
        for head in range(heads):
            attend(head, now)
            if later is not None:
                project(col + 1, head, later)
        close(col, now)

    def two_columns(step, carry):
        column(2 * step, first_set, second_set)
        column(2 * step + 1, second_set, first_set)
        return carry

    lax.fori_loop(0, (per - 1) // 2, two_columns, 0)
    if per % 2 == 0:
        column(per - 2, first_set, second_set)
        column(per - 1, second_set)
    else:
        column(per - 1, first_set)

    @pl.when(jnp.min(fine_ref[...]) < 0.5)
    def _():
        tile = 128
        query_ref, key_ref, value_ref, gate_ref, total_ref = first_set

        def exact(col, carry):
            for part in range(heads):
                project(col, part, first_set, hide=False)
            first = (lax.broadcasted_iota(jnp.int32, (8, channels), 1) == 0).astype(jnp.bfloat16)
            lift = NEG_BIG * (dot_nt(first, value_ref[:, channels:])[:1] - 1.0)

            def rows_exact(step, inner):
                rows = pl.ds(pl.multiple_of(step * tile, tile), tile)
                for head in range(heads):
                    low = head * head_dim
                    scores = dot_nt(query_ref[rows, :] * own[head], key_ref[...])
                    scores = scores + bias_ref[head, rows, :].astype(jnp.float32) + lift
                    probs = jnp.exp(scores - jnp.max(scores, axis=1, keepdims=True))
                    totals = jnp.sum(probs, axis=1, keepdims=True)
                    attended = dot(probs.astype(jnp.bfloat16), value_ref[:, :channels]) / totals
                    total_ref[rows, low : low + head_dim] = attended[:, low : low + head_dim]
                return inner

            lax.fori_loop(0, width // tile, rows_exact, 0)
            result_ref[pl.ds(col, width, stride=per), :] = total_ref[:, :channels] * gate_ref[...].astype(jnp.float32)
            return carry

        lax.fori_loop(0, per, exact, 0)

    out_ref[...] = result_ref[...].astype(jnp.bfloat16)


def finish_kernel(rows, width, groups, chunks, *refs):
    chunk_refs = refs[:chunks]
    out_weight_ref, out_offset_ref, update_ref = refs[chunks : chunks + 3]
    wide_refs = refs[chunks + 3 : 2 * chunks + 3]
    row_ref = refs[2 * chunks + 3]
    cols = width // groups
    per = cols // chunks
    for chunk in range(chunks):
        wide_refs[chunk][...] = dot(chunk_refs[chunk][...], out_weight_ref[...]) + out_offset_ref[...]
    for row in range(rows):
        for col in range(cols):
            chunk, place = divmod(col, per)
            row_ref[row % 2, pl.ds(col, groups, stride=cols), :] = wide_refs[chunk][
                pl.ds(row * per + place, groups, stride=rows * per), :
            ]
        update_ref[pl.ds(row * width, width), :] = row_ref[row % 2].astype(jnp.bfloat16)


def local(
    pair,
    pair_mask,
    ln_gain,
    ln_offset,
    bias_weight,
    query_weight,
    key_weight,
    value_weight,
    gate_weight,
    gate_offset,
    out_weight,
    out_offset,
):
    rows, width, channels = pair.shape
    groups = lax.axis_size("dap")
    cols = width // groups
    per = cols // CHUNKS
    heads = bias_weight.shape[1]
    block = groups * rows * per
    low, wide = jnp.bfloat16, jnp.float32
    params = pltpu.CompilerParams(vmem_limit_bytes=60 * 1024 * 1024)
    normed, bias_copies = pl.pallas_call(
        functools.partial(norm_kernel, rows, width, heads),
        out_shape=[
            jax.ShapeDtypeStruct((rows * width, channels), low),
            jax.ShapeDtypeStruct((FIRST * rows * heads, width), low),
        ],
        in_specs=in_vmem(4),
        out_specs=in_vmem(2),
        scratch_shapes=[pltpu.VMEM((rows * heads, width), wide)],
        compiler_params=params,
        name="norm",
    )(pair.reshape(rows * width, channels), ln_gain.reshape(1, channels), ln_offset.reshape(1, channels), bias_weight.T)
    *sends, present, packed = pl.pallas_call(
        functools.partial(layout_kernel, rows, width, groups, CHUNKS),
        out_shape=[jax.ShapeDtypeStruct((block, channels), low)] * CHUNKS
        + [jax.ShapeDtypeStruct((width, cols), low), jax.ShapeDtypeStruct((channels, 4 * channels), low)],
        in_specs=in_vmem(6),
        out_specs=in_vmem(CHUNKS + 2),
        scratch_shapes=[pltpu.VMEM((2, width, channels), wide)] + [pltpu.VMEM((block, channels), wide)] * CHUNKS,
        compiler_params=params,
        cost_estimate=pl.CostEstimate(flops=10**6, bytes_accessed=15 * 10**6, transcendentals=0),
        name="layout",
    )(normed, pair_mask.T, query_weight, key_weight, value_weight, gate_weight)

    pieces, sends = gather_bias(bias_copies, sends)
    whole = pl.BlockSpec(memory_space=pl.ANY)
    later = sends[1:]
    turned, *later = pl.pallas_call(
        functools.partial(turn_kernel, heads, rows, len(later)),
        out_shape=[jax.ShapeDtypeStruct((heads, width, width), low)]
        + [jax.ShapeDtypeStruct(one.shape, one.dtype) for one in later],
        in_specs=in_vmem(len(pieces)) + [whole] * len(later),
        out_specs=in_vmem(1) + [whole] * len(later),
        input_output_aliases={len(pieces) + at: 1 + at for at in range(len(later))},
        scratch_shapes=[pltpu.VMEM((width // channels, width * heads, channels), wide)],
        compiler_params=pltpu.CompilerParams(vmem_limit_bytes=TURN_MIB * 1024 * 1024),
        name="turn",
    )(*pieces, *later)
    moved = [
        lax.all_to_all(
            send.reshape(groups, rows * per, channels), "dap", split_axis=0, concat_axis=0, tiled=True
        ).reshape(block, channels)
        for send in (sends[0], *later)
    ]

    returned = []
    for chunk in range(CHUNKS):
        gated = pl.pallas_call(
            functools.partial(attend_kernel, chunk, per, heads),
            out_shape=jax.ShapeDtypeStruct((block, channels), low),
            in_specs=in_vmem(5),
            out_specs=in_vmem(1)[0],
            scratch_shapes=[
                pltpu.VMEM((block, channels), wide),
                pltpu.VMEM((block, channels), wide),
                pltpu.VMEM((8, channels), wide),
            ]
            + 2
            * [
                pltpu.VMEM((width, channels), low),
                pltpu.VMEM((width, channels), low),
                pltpu.VMEM((width, 2 * channels), low),
                pltpu.VMEM((width, channels), low),
                pltpu.VMEM((width, 2 * channels), wide),
            ],
            compiler_params=pltpu.CompilerParams(vmem_limit_bytes=ATTEND_MIB * 1024 * 1024),
            cost_estimate=pl.CostEstimate(
                flops=per * heads * width * width * channels * 6,
                bytes_accessed=2 * heads * width * width,
                transcendentals=per * heads * width * width,
            ),
            name="attend",
        )(
            moved[chunk],
            turned,
            present,
            packed,
            gate_offset.reshape(1, channels),
        )
        returned.append(
            lax.all_to_all(
                gated.reshape(groups, rows * per, channels), "dap", split_axis=0, concat_axis=0, tiled=True
            ).reshape(block, channels)
        )
    update = pl.pallas_call(
        functools.partial(finish_kernel, rows, width, groups, CHUNKS),
        out_shape=jax.ShapeDtypeStruct((rows * width, channels), low),
        in_specs=in_vmem(CHUNKS + 2),
        out_specs=in_vmem(1)[0],
        scratch_shapes=[pltpu.VMEM((block, channels), wide)] * CHUNKS + [pltpu.VMEM((2, width, channels), wide)],
        compiler_params=params,
        name="finish",
    )(*returned, out_weight, out_offset.reshape(1, channels))
    return update.reshape(rows, width, channels)


def solution(mesh):
    in_specs = (P(("dp", "dap"), None, None), P("dp", "dap")) + (P(),) * 10
    out_specs = P(("dp", "dap"), None, None)
    return jax.shard_map(local, mesh=mesh, in_specs=in_specs, out_specs=out_specs, check_vma=False)
```

```python
import functools

import jax
import jax.numpy as jnp
from jax import lax
from jax.experimental import pallas as pl
from jax.experimental.pallas import tpu as pltpu
from jax.sharding import PartitionSpec as P

NEG_BIG = 1000000000.0
EPSILON = 1e-05
CHUNKS = 2
ATTEND_MIB = 40
TURN_MIB = 60
FINISH_MIB = 30
TOTAL_LOW = 1e-20
TOTAL_HIGH = 1e30
NT = (((1,), (1,)), ((), ()))
PLACE = ("z", "y", "x", "core")
PLACE_SIZES = (2, 4, 4, 2)
TOTAL = 64
FIRST = 8
SHIFTS = (0, 1, 2, 3)


def dot(lhs, rhs):
    return jnp.dot(lhs, rhs, preferred_element_type=jnp.float32)


def dot_nt(lhs, rhs):
    return lax.dot_general(lhs, rhs, NT, preferred_element_type=jnp.float32)


def in_vmem(count):
    return [pl.BlockSpec(memory_space=pltpu.VMEM)] * count


def norm_kernel(rows, width, heads, pair_ref, gain_ref, offset_ref, bias_weight_ref, normed_ref, bias_ref, wide_ref):
    weight = bias_weight_ref[...]
    blank = jnp.zeros_like(weight)
    both = jnp.concatenate(
        [jnp.concatenate([weight, blank], axis=1), jnp.concatenate([blank, weight], axis=1)], axis=0
    )
    for row in range(rows):
        wide = pair_ref[pl.ds(row * width, width), :].astype(jnp.float32)
        centred = wide - jnp.mean(wide, axis=1, keepdims=True)
        spread = jnp.mean(centred * centred, axis=1, keepdims=True)
        normed = centred * lax.rsqrt(spread + EPSILON) * gain_ref[...] + offset_ref[...]
        normed_ref[pl.ds(row * width, width), :] = normed.astype(jnp.bfloat16)
        if row % 2:
            two = [normed_ref[pl.ds(at * width, width), :] for at in (row - 1, row)]
            wide_ref[pl.ds((row - 1) * heads, 2 * heads), :] = dot_nt(both, jnp.concatenate(two, axis=1))
    for copy in range(bias_ref.shape[0] // (rows * heads)):
        bias_ref[pl.ds(copy * rows * heads, rows * heads), :] = wide_ref[...].astype(jnp.bfloat16)


def layout_kernel(rows, width, groups, chunks, normed_ref, mask_ref, *refs):
    weight_refs, chunk_refs = refs[:4], refs[4 : 4 + chunks]
    present_ref, packed_ref, wide_ref = refs[4 + chunks : 7 + chunks]
    staged_refs = refs[7 + chunks :]
    cols = width // groups
    per = cols // chunks
    for row in range(rows):
        wide_ref[row % 2] = normed_ref[pl.ds(row * width, width), :].astype(jnp.float32)
        for col in range(cols):
            chunk, place = divmod(col, per)
            staged_refs[chunk][pl.ds(row * per + place, groups, stride=rows * per), :] = wide_ref[
                row % 2, pl.ds(col, groups, stride=cols), :
            ]
    for chunk in range(chunks):
        chunk_refs[chunk][...] = staged_refs[chunk][...].astype(jnp.bfloat16)
    present_ref[...] = mask_ref[...].astype(jnp.float32).T.astype(jnp.bfloat16)
    channels = normed_ref.shape[1]
    for at, ref in enumerate(weight_refs):
        packed_ref[:, at * channels : (at + 1) * channels] = ref[...]


def hold_kernel(*refs):
    pass


def hold(*arrays):
    whole = [pl.BlockSpec(memory_space=pl.ANY)] * len(arrays)
    return pl.pallas_call(
        hold_kernel,
        out_shape=[jax.ShapeDtypeStruct(one.shape, one.dtype) for one in arrays],
        in_specs=whole,
        out_specs=whole,
        input_output_aliases={at: at for at in range(len(arrays))},
        name="hold",
    )(*arrays)


def place_of(index):
    place = {}
    for axis, size in zip(reversed(PLACE), reversed(PLACE_SIZES)):
        place[axis] = index % size if isinstance(index, int) else lax.rem(index, size)
        index = index // size
    return place


def index_of(place):
    index = 0
    for axis, size in zip(PLACE, PLACE_SIZES):
        index = index * size + place[axis]
    return index


ORDER = (("y", "x"), ("x", "y"))


def first_groups():
    groups = {}
    for index in range(TOTAL):
        place = place_of(index)
        groups.setdefault((place["core"], place[ORDER[place["core"]][1]]), []).append(index)
    return list(groups.values())


def second_pairs(step):
    pairs = []
    for index in range(TOTAL):
        place = place_of(index)
        axis = ORDER[place["core"]][1]
        pairs.append((index, index_of({**place, axis: (place[axis] + step) % 4})))
    return pairs


def gather_bias(bias_copies, sends):
    first = lax.all_to_all(
        bias_copies.reshape((FIRST, bias_copies.shape[0] // FIRST, bias_copies.shape[1])),
        "dap",
        split_axis=0,
        concat_axis=0,
        axis_index_groups=first_groups(),
        tiled=True,
    ).reshape(bias_copies.shape)
    first, *sends = hold(first, *sends)
    pieces = [first if step == 0 else lax.ppermute(first, "dap", second_pairs(step)) for step in SHIFTS]
    other_core = [(index, index ^ 1) for index in range(TOTAL)]
    return pieces + [lax.ppermute(piece, "dap", other_core) for piece in pieces], sends


def turn_kernel(heads, rows, handed, *refs):
    count = 2 * len(SHIFTS)
    pieces, turned_ref, wide_ref = refs[:count], refs[count + handed], refs[-1]
    width = turned_ref.shape[1]
    tile = wide_ref.shape[2]
    here = place_of(lax.axis_index("dap"))
    block = rows * heads

    def unpack(core, my_pieces):
        first, second = ORDER[core]
        for far, step in enumerate(SHIFTS):
            for place in range(FIRST):
                at = {
                    "z": place // 4,
                    "core": core,
                    first: place % 4,
                    second: lax.rem(here[second] + 4 - step, 4),
                }
                start = pl.multiple_of(index_of(at) * block, 16)
                for lane in range(width // tile):
                    wide_ref[lane, pl.ds(start, block), :] = my_pieces[far][
                        pl.ds(place * block, block), lane * tile : (lane + 1) * tile
                    ].astype(jnp.float32)

    for core in range(2):

        @pl.when(here["core"] == core)
        def _():
            unpack(core, pieces[: len(SHIFTS)])
            unpack(1 - core, pieces[len(SHIFTS) :])

    unit = (
        lax.broadcasted_iota(jnp.int32, (tile, tile), 0) == lax.broadcasted_iota(jnp.int32, (tile, tile), 1)
    ).astype(jnp.bfloat16)
    for head in range(heads):
        for at in range(0, width, tile):
            one = wide_ref[at // tile, pl.ds(head, width, stride=heads), :].astype(jnp.bfloat16)
            turned_ref[head, pl.ds(at, tile), :] = dot_nt(unit, one).astype(jnp.bfloat16)


def attend_kernel(
    chunk,
    per,
    heads,
    moved_ref,
    bias_ref,
    present_ref,
    weight_ref,
    gate_offset_ref,
    out_ref,
    source_ref,
    result_ref,
    fine_ref,
    *sets,
):
    channels = moved_ref.shape[1]
    width, mask_cols = present_ref.shape
    head_dim = channels // heads
    source_ref[...] = moved_ref[...].astype(jnp.float32)
    lane_head = lax.broadcasted_iota(jnp.int32, (1, channels), 1) // head_dim
    own = [(lane_head == head).astype(jnp.bfloat16) for head in range(heads)]
    fine_ref[...] = jnp.ones_like(fine_ref)
    share = width // heads
    first_set, second_set = sets[:5], sets[5:]

    def project(col, part, buffers, hide=True):
        query_ref, key_ref, value_ref, gate_ref, _ = buffers
        rows = pl.ds(part * share, share)
        source = source_ref[pl.ds(col + part * share * per, share, stride=per), :].astype(jnp.bfloat16)
        wide = dot(source, weight_ref[...])
        query_ref[rows, :] = (wide[:, :channels] * head_dim ** (-0.5)).astype(jnp.bfloat16)
        key_ref[rows, :] = wide[:, channels : 2 * channels].astype(jnp.bfloat16)
        pick = (lax.broadcasted_iota(jnp.int32, (mask_cols, channels), 0) == chunk * per + col).astype(jnp.bfloat16)
        present = dot(present_ref[rows, :], pick).astype(jnp.bfloat16)
        values = wide[:, 2 * channels : 3 * channels].astype(jnp.bfloat16)
        value_ref[rows, :channels] = values * present if hide else values
        value_ref[rows, channels:] = present
        gate_ref[rows, :] = jax.nn.sigmoid(wide[:, 3 * channels :] + gate_offset_ref[...]).astype(jnp.bfloat16)

    def attend(head, buffers):
        query_ref, key_ref, value_ref, _, total_ref = buffers
        scores = dot_nt(query_ref[...] * own[head], key_ref[...]) + bias_ref[head].astype(jnp.float32)
        total = dot(jnp.exp(scores).astype(jnp.bfloat16), value_ref[...])
        for low in (head * head_dim, channels + head * head_dim):
            total_ref[:, low : low + head_dim] = total[:, low : low + head_dim]

    def close(col, buffers):
        _, _, _, gate_ref, total_ref = buffers
        sums = total_ref[:, channels:]
        fine = jnp.where((sums > TOTAL_LOW) & (sums < TOTAL_HIGH), 1.0, 0.0)
        fine_ref[...] = jnp.minimum(fine_ref[...], jnp.min(fine.reshape(width // 8, 8, channels), axis=0))
        result_ref[pl.ds(col, width, stride=per), :] = (
            total_ref[:, :channels] / sums * gate_ref[...].astype(jnp.float32)
        )

    for part in range(heads):
        project(0, part, first_set)

    def column(col, now, later=None):
        for head in range(heads):
            attend(head, now)
            if later is not None:
                project(col + 1, head, later)
        close(col, now)

    def two_columns(step, carry):
        column(2 * step, first_set, second_set)
        column(2 * step + 1, second_set, first_set)
        return carry

    lax.fori_loop(0, (per - 1) // 2, two_columns, 0)
    if per % 2 == 0:
        column(per - 2, first_set, second_set)
        column(per - 1, second_set)
    else:
        column(per - 1, first_set)

    @pl.when(jnp.min(fine_ref[...]) < 0.5)
    def _():
        tile = 128
        query_ref, key_ref, value_ref, gate_ref, total_ref = first_set

        def exact(col, carry):
            for part in range(heads):
                project(col, part, first_set, hide=False)
            first = (lax.broadcasted_iota(jnp.int32, (8, channels), 1) == 0).astype(jnp.bfloat16)
            lift = NEG_BIG * (dot_nt(first, value_ref[:, channels:])[:1] - 1.0)

            def rows_exact(step, inner):
                rows = pl.ds(pl.multiple_of(step * tile, tile), tile)
                for head in range(heads):
                    low = head * head_dim
                    scores = dot_nt(query_ref[rows, :] * own[head], key_ref[...])
                    scores = scores + bias_ref[head, rows, :].astype(jnp.float32) + lift
                    probs = jnp.exp(scores - jnp.max(scores, axis=1, keepdims=True))
                    totals = jnp.sum(probs, axis=1, keepdims=True)
                    attended = dot(probs.astype(jnp.bfloat16), value_ref[:, :channels]) / totals
                    total_ref[rows, low : low + head_dim] = attended[:, low : low + head_dim]
                return inner

            lax.fori_loop(0, width // tile, rows_exact, 0)
            result_ref[pl.ds(col, width, stride=per), :] = total_ref[:, :channels] * gate_ref[...].astype(jnp.float32)
            return carry

        lax.fori_loop(0, per, exact, 0)

    out_ref[...] = result_ref[...].astype(jnp.bfloat16)


def finish_kernel(rows, width, groups, chunks, *refs):
    chunk_refs = refs[:chunks]
    out_weight_ref, out_offset_ref, update_ref = refs[chunks : chunks + 3]
    wide_refs = refs[chunks + 3 : 2 * chunks + 3]
    row_ref = refs[2 * chunks + 3]
    cols = width // groups
    per = cols // chunks
    for chunk in range(chunks):
        wide_refs[chunk][...] = dot(chunk_refs[chunk][...], out_weight_ref[...]) + out_offset_ref[...]
    for row in range(rows):
        for col in range(cols):
            chunk, place = divmod(col, per)
            row_ref[row % 2, pl.ds(col, groups, stride=cols), :] = wide_refs[chunk][
                pl.ds(row * per + place, groups, stride=rows * per), :
            ]
        update_ref[pl.ds(row * width, width), :] = row_ref[row % 2].astype(jnp.bfloat16)


def local(
    pair,
    pair_mask,
    ln_gain,
    ln_offset,
    bias_weight,
    query_weight,
    key_weight,
    value_weight,
    gate_weight,
    gate_offset,
    out_weight,
    out_offset,
):
    rows, width, channels = pair.shape
    groups = lax.axis_size("dap")
    cols = width // groups
    per = cols // CHUNKS
    heads = bias_weight.shape[1]
    block = groups * rows * per
    low, wide = jnp.bfloat16, jnp.float32
    params = pltpu.CompilerParams(vmem_limit_bytes=60 * 1024 * 1024)
    normed, bias_copies = pl.pallas_call(
        functools.partial(norm_kernel, rows, width, heads),
        out_shape=[
            jax.ShapeDtypeStruct((rows * width, channels), low),
            jax.ShapeDtypeStruct((FIRST * rows * heads, width), low),
        ],
        in_specs=in_vmem(4),
        out_specs=in_vmem(2),
        scratch_shapes=[pltpu.VMEM((rows * heads, width), wide)],
        compiler_params=params,
        name="norm",
    )(pair.reshape(rows * width, channels), ln_gain.reshape(1, channels), ln_offset.reshape(1, channels), bias_weight.T)
    *sends, present, packed = pl.pallas_call(
        functools.partial(layout_kernel, rows, width, groups, CHUNKS),
        out_shape=[jax.ShapeDtypeStruct((block, channels), low)] * CHUNKS
        + [jax.ShapeDtypeStruct((width, cols), low), jax.ShapeDtypeStruct((channels, 4 * channels), low)],
        in_specs=in_vmem(6),
        out_specs=in_vmem(CHUNKS + 2),
        scratch_shapes=[pltpu.VMEM((2, width, channels), wide)] + [pltpu.VMEM((block, channels), wide)] * CHUNKS,
        compiler_params=params,
        cost_estimate=pl.CostEstimate(flops=10**6, bytes_accessed=15 * 10**6, transcendentals=0),
        name="layout",
    )(normed, pair_mask.T, query_weight, key_weight, value_weight, gate_weight)

    pieces, sends = gather_bias(bias_copies, sends)
    whole = pl.BlockSpec(memory_space=pl.ANY)
    later = sends[1:]
    turned, *later = pl.pallas_call(
        functools.partial(turn_kernel, heads, rows, len(later)),
        out_shape=[jax.ShapeDtypeStruct((heads, width, width), low)]
        + [jax.ShapeDtypeStruct(one.shape, one.dtype) for one in later],
        in_specs=in_vmem(len(pieces)) + [whole] * len(later),
        out_specs=in_vmem(1) + [whole] * len(later),
        input_output_aliases={len(pieces) + at: 1 + at for at in range(len(later))},
        scratch_shapes=[pltpu.VMEM((width // channels, width * heads, channels), wide)],
        compiler_params=pltpu.CompilerParams(vmem_limit_bytes=TURN_MIB * 1024 * 1024),
        name="turn",
    )(*pieces, *later)
    moved = [
        lax.all_to_all(
            send.reshape(groups, rows * per, channels), "dap", split_axis=0, concat_axis=0, tiled=True
        ).reshape(block, channels)
        for send in (sends[0], *later)
    ]

    returned = []
    for chunk in range(CHUNKS):
        gated = pl.pallas_call(
            functools.partial(attend_kernel, chunk, per, heads),
            out_shape=jax.ShapeDtypeStruct((block, channels), low),
            in_specs=in_vmem(5),
            out_specs=in_vmem(1)[0],
            scratch_shapes=[
                pltpu.VMEM((block, channels), wide),
                pltpu.VMEM((block, channels), wide),
                pltpu.VMEM((8, channels), wide),
            ]
            + 2
            * [
                pltpu.VMEM((width, channels), low),
                pltpu.VMEM((width, channels), low),
                pltpu.VMEM((width, 2 * channels), low),
                pltpu.VMEM((width, channels), low),
                pltpu.VMEM((width, 2 * channels), wide),
            ],
            compiler_params=pltpu.CompilerParams(vmem_limit_bytes=ATTEND_MIB * 1024 * 1024),
            cost_estimate=pl.CostEstimate(
                flops=per * heads * width * width * channels * 6,
                bytes_accessed=2 * heads * width * width,
                transcendentals=per * heads * width * width,
            ),
            name="attend",
        )(
            moved[chunk],
            turned,
            present,
            packed,
            gate_offset.reshape(1, channels),
        )
        returned.append(
            lax.all_to_all(
                gated.reshape(groups, rows * per, channels), "dap", split_axis=0, concat_axis=0, tiled=True
            ).reshape(block, channels)
        )
    update = pl.pallas_call(
        functools.partial(finish_kernel, rows, width, groups, CHUNKS),
        out_shape=jax.ShapeDtypeStruct((rows * width, channels), low),
        in_specs=in_vmem(CHUNKS + 2),
        out_specs=in_vmem(1)[0],
        scratch_shapes=[pltpu.VMEM((block, channels), wide)] * CHUNKS + [pltpu.VMEM((2, width, channels), wide)],
        compiler_params=pltpu.CompilerParams(vmem_limit_bytes=FINISH_MIB * 1024 * 1024),
        name="finish",
    )(*returned, out_weight, out_offset.reshape(1, channels))
    return update.reshape(rows, width, channels)


def solution(mesh):
    in_specs = (P(("dp", "dap"), None, None), P("dp", "dap")) + (P(),) * 10
    out_specs = P(("dp", "dap"), None, None)
    return jax.shard_map(local, mesh=mesh, in_specs=in_specs, out_specs=out_specs, check_vma=False)
```

```python
import functools

import jax
import jax.numpy as jnp
from jax import lax
from jax.experimental import pallas as pl
from jax.experimental.pallas import tpu as pltpu
from jax.sharding import PartitionSpec as P

NEG_BIG = 1000000000.0
EPSILON = 1e-05
CHUNKS = 2
ATTEND_MIB = 40
TURN_MIB = 60
FINISH_MIB = 30
TOTAL_LOW = 1e-20
TOTAL_HIGH = 1e30
NT = (((1,), (1,)), ((), ()))
PLACE = ("z", "y", "x", "core")
PLACE_SIZES = (2, 4, 4, 2)
TOTAL = 64
FIRST = 8
SHIFTS = (0, 1, 2, 3)


def dot(lhs, rhs):
    return jnp.dot(lhs, rhs, preferred_element_type=jnp.float32)


def dot_nt(lhs, rhs):
    return lax.dot_general(lhs, rhs, NT, preferred_element_type=jnp.float32)


def in_vmem(count):
    return [pl.BlockSpec(memory_space=pltpu.VMEM)] * count


def norm_kernel(rows, width, heads, pair_ref, gain_ref, offset_ref, bias_weight_ref, normed_ref, bias_ref, wide_ref):
    weight = bias_weight_ref[...]
    blank = jnp.zeros_like(weight)
    both = jnp.concatenate(
        [jnp.concatenate([weight, blank], axis=1), jnp.concatenate([blank, weight], axis=1)], axis=0
    )
    for row in range(rows):
        wide = pair_ref[pl.ds(row * width, width), :].astype(jnp.float32)
        centred = wide - jnp.mean(wide, axis=1, keepdims=True)
        spread = jnp.mean(centred * centred, axis=1, keepdims=True)
        normed = centred * lax.rsqrt(spread + EPSILON) * gain_ref[...] + offset_ref[...]
        normed_ref[pl.ds(row * width, width), :] = normed.astype(jnp.bfloat16)
        if row % 2:
            two = [normed_ref[pl.ds(at * width, width), :] for at in (row - 1, row)]
            wide_ref[pl.ds((row - 1) * heads, 2 * heads), :] = dot_nt(both, jnp.concatenate(two, axis=1))
    for copy in range(bias_ref.shape[0] // (rows * heads)):
        bias_ref[pl.ds(copy * rows * heads, rows * heads), :] = wide_ref[...].astype(jnp.bfloat16)


def layout_kernel(rows, width, groups, chunks, normed_ref, mask_ref, *refs):
    weight_refs, chunk_refs = refs[:4], refs[4 : 4 + chunks]
    present_ref, packed_ref, wide_ref = refs[4 + chunks : 7 + chunks]
    staged_refs = refs[7 + chunks :]
    cols = width // groups
    per = cols // chunks
    for row in range(rows):
        wide_ref[row % 2] = normed_ref[pl.ds(row * width, width), :].astype(jnp.float32)
        for col in range(cols):
            chunk, place = divmod(col, per)
            staged_refs[chunk][pl.ds(row * per + place, groups, stride=rows * per), :] = wide_ref[
                row % 2, pl.ds(col, groups, stride=cols), :
            ]
    for chunk in range(chunks):
        chunk_refs[chunk][...] = staged_refs[chunk][...].astype(jnp.bfloat16)
    present_ref[...] = mask_ref[...].astype(jnp.float32).T.astype(jnp.bfloat16)
    channels = normed_ref.shape[1]
    for at, ref in enumerate(weight_refs):
        packed_ref[:, at * channels : (at + 1) * channels] = ref[...]


def hold_kernel(*refs):
    pass


def hold(*arrays):
    whole = [pl.BlockSpec(memory_space=pl.ANY)] * len(arrays)
    return pl.pallas_call(
        hold_kernel,
        out_shape=[jax.ShapeDtypeStruct(one.shape, one.dtype) for one in arrays],
        in_specs=whole,
        out_specs=whole,
        input_output_aliases={at: at for at in range(len(arrays))},
        name="hold",
    )(*arrays)


def place_of(index):
    place = {}
    for axis, size in zip(reversed(PLACE), reversed(PLACE_SIZES)):
        place[axis] = index % size if isinstance(index, int) else lax.rem(index, size)
        index = index // size
    return place


def index_of(place):
    index = 0
    for axis, size in zip(PLACE, PLACE_SIZES):
        index = index * size + place[axis]
    return index


ORDER = (("y", "x"), ("x", "y"))


def first_groups():
    groups = {}
    for index in range(TOTAL):
        place = place_of(index)
        groups.setdefault((place["core"], place[ORDER[place["core"]][1]]), []).append(index)
    return list(groups.values())


def second_pairs(step):
    pairs = []
    for index in range(TOTAL):
        place = place_of(index)
        axis = ORDER[place["core"]][1]
        pairs.append((index, index_of({**place, axis: (place[axis] + step) % 4})))
    return pairs


def gather_bias(bias_copies, sends):
    first = lax.all_to_all(
        bias_copies.reshape((FIRST, bias_copies.shape[0] // FIRST, bias_copies.shape[1])),
        "dap",
        split_axis=0,
        concat_axis=0,
        axis_index_groups=first_groups(),
        tiled=True,
    ).reshape(bias_copies.shape)
    first, *sends = hold(first, *sends)
    pieces = [first if step == 0 else lax.ppermute(first, "dap", second_pairs(step)) for step in SHIFTS]
    other_core = [(index, index ^ 1) for index in range(TOTAL)]
    return pieces + [lax.ppermute(piece, "dap", other_core) for piece in pieces], sends


def turn_kernel(heads, rows, handed, *refs):
    count = 2 * len(SHIFTS)
    pieces, turned_ref, wide_ref = refs[:count], refs[count + handed], refs[-1]
    width = turned_ref.shape[1]
    tile = wide_ref.shape[2]
    here = place_of(lax.axis_index("dap"))
    block = rows * heads

    for other in range(2):
        core = here["core"] if other == 0 else 1 - here["core"]
        last = jnp.where(core == 0, here["x"], here["y"])
        for far, step in enumerate(SHIFTS):
            second = lax.rem(last + 4 - step, 4)
            for place in range(FIRST):
                first = place % 4
                at = {
                    "z": place // 4,
                    "y": jnp.where(core == 0, first, second),
                    "x": jnp.where(core == 0, second, first),
                    "core": core,
                }
                start = pl.multiple_of(index_of(at) * block, 16)
                for lane in range(width // tile):
                    wide_ref[lane, pl.ds(start, block), :] = pieces[other * len(SHIFTS) + far][
                        pl.ds(place * block, block), lane * tile : (lane + 1) * tile
                    ].astype(jnp.float32)

    unit = (
        lax.broadcasted_iota(jnp.int32, (tile, tile), 0) == lax.broadcasted_iota(jnp.int32, (tile, tile), 1)
    ).astype(jnp.bfloat16)
    for head in range(heads):
        for at in range(0, width, tile):
            one = wide_ref[at // tile, pl.ds(head, width, stride=heads), :].astype(jnp.bfloat16)
            turned_ref[head, pl.ds(at, tile), :] = dot_nt(unit, one).astype(jnp.bfloat16)


def attend_kernel(
    chunk,
    per,
    heads,
    moved_ref,
    bias_ref,
    present_ref,
    weight_ref,
    gate_offset_ref,
    out_ref,
    source_ref,
    result_ref,
    fine_ref,
    *sets,
):
    channels = moved_ref.shape[1]
    width, mask_cols = present_ref.shape
    head_dim = channels // heads
    source_ref[...] = moved_ref[...].astype(jnp.float32)
    lane_head = lax.broadcasted_iota(jnp.int32, (1, channels), 1) // head_dim
    own = [(lane_head == head).astype(jnp.bfloat16) for head in range(heads)]
    fine_ref[...] = jnp.ones_like(fine_ref)
    share = width // heads
    first_set, second_set = sets[:5], sets[5:]

    def project(col, part, buffers, hide=True):
        query_ref, key_ref, value_ref, gate_ref, _ = buffers
        rows = pl.ds(part * share, share)
        source = source_ref[pl.ds(col + part * share * per, share, stride=per), :].astype(jnp.bfloat16)
        wide = dot(source, weight_ref[...])
        query_ref[rows, :] = (wide[:, :channels] * head_dim ** (-0.5)).astype(jnp.bfloat16)
        key_ref[rows, :] = wide[:, channels : 2 * channels].astype(jnp.bfloat16)
        pick = (lax.broadcasted_iota(jnp.int32, (mask_cols, channels), 0) == chunk * per + col).astype(jnp.bfloat16)
        present = dot(present_ref[rows, :], pick).astype(jnp.bfloat16)
        values = wide[:, 2 * channels : 3 * channels].astype(jnp.bfloat16)
        value_ref[rows, :channels] = values * present if hide else values
        value_ref[rows, channels:] = present
        gate_ref[rows, :] = jax.nn.sigmoid(wide[:, 3 * channels :] + gate_offset_ref[...]).astype(jnp.bfloat16)

    def attend(head, buffers):
        query_ref, key_ref, value_ref, _, total_ref = buffers
        scores = dot_nt(query_ref[...] * own[head], key_ref[...]) + bias_ref[head].astype(jnp.float32)
        total = dot(jnp.exp(scores).astype(jnp.bfloat16), value_ref[...])
        for low in (head * head_dim, channels + head * head_dim):
            total_ref[:, low : low + head_dim] = total[:, low : low + head_dim]

    def close(col, buffers):
        _, _, _, gate_ref, total_ref = buffers
        sums = total_ref[:, channels:]
        fine = jnp.where((sums > TOTAL_LOW) & (sums < TOTAL_HIGH), 1.0, 0.0)
        fine_ref[...] = jnp.minimum(fine_ref[...], jnp.min(fine.reshape(width // 8, 8, channels), axis=0))
        result_ref[pl.ds(col, width, stride=per), :] = (
            total_ref[:, :channels] / sums * gate_ref[...].astype(jnp.float32)
        )

    for part in range(heads):
        project(0, part, first_set)

    def two_columns(step, carry):
        for now, later, col in ((first_set, second_set, 2 * step), (second_set, first_set, 2 * step + 1)):
            for head in range(heads):
                attend(head, now)
                project(jnp.minimum(col + 1, per - 1), head, later)
            close(col, now)
        return carry

    lax.fori_loop(0, per // 2, two_columns, 0)

    @pl.when(jnp.min(fine_ref[...]) < 0.5)
    def _():
        tile = 128
        query_ref, key_ref, value_ref, gate_ref, total_ref = first_set

        def exact(col, carry):
            for part in range(heads):
                project(col, part, first_set, hide=False)
            first = (lax.broadcasted_iota(jnp.int32, (8, channels), 1) == 0).astype(jnp.bfloat16)
            lift = NEG_BIG * (dot_nt(first, value_ref[:, channels:])[:1] - 1.0)

            def rows_exact(step, inner):
                rows = pl.ds(pl.multiple_of(step * tile, tile), tile)
                for head in range(heads):
                    low = head * head_dim
                    scores = dot_nt(query_ref[rows, :] * own[head], key_ref[...])
                    scores = scores + bias_ref[head, rows, :].astype(jnp.float32) + lift
                    probs = jnp.exp(scores - jnp.max(scores, axis=1, keepdims=True))
                    totals = jnp.sum(probs, axis=1, keepdims=True)
                    attended = dot(probs.astype(jnp.bfloat16), value_ref[:, :channels]) / totals
                    total_ref[rows, low : low + head_dim] = attended[:, low : low + head_dim]
                return inner

            lax.fori_loop(0, width // tile, rows_exact, 0)
            result_ref[pl.ds(col, width, stride=per), :] = total_ref[:, :channels] * gate_ref[...].astype(jnp.float32)
            return carry

        lax.fori_loop(0, per, exact, 0)

    out_ref[...] = result_ref[...].astype(jnp.bfloat16)


def finish_kernel(rows, width, groups, chunks, *refs):
    chunk_refs = refs[:chunks]
    out_weight_ref, out_offset_ref, update_ref = refs[chunks : chunks + 3]
    wide_refs = refs[chunks + 3 : 2 * chunks + 3]
    row_ref = refs[2 * chunks + 3]
    cols = width // groups
    per = cols // chunks
    for chunk in range(chunks):
        wide_refs[chunk][...] = dot(chunk_refs[chunk][...], out_weight_ref[...]) + out_offset_ref[...]
    for row in range(rows):
        for col in range(cols):
            chunk, place = divmod(col, per)
            row_ref[row % 2, pl.ds(col, groups, stride=cols), :] = wide_refs[chunk][
                pl.ds(row * per + place, groups, stride=rows * per), :
            ]
        update_ref[pl.ds(row * width, width), :] = row_ref[row % 2].astype(jnp.bfloat16)


def local(
    pair,
    pair_mask,
    ln_gain,
    ln_offset,
    bias_weight,
    query_weight,
    key_weight,
    value_weight,
    gate_weight,
    gate_offset,
    out_weight,
    out_offset,
):
    rows, width, channels = pair.shape
    groups = lax.axis_size("dap")
    cols = width // groups
    per = cols // CHUNKS
    heads = bias_weight.shape[1]
    block = groups * rows * per
    low, wide = jnp.bfloat16, jnp.float32
    params = pltpu.CompilerParams(vmem_limit_bytes=60 * 1024 * 1024)
    normed, bias_copies = pl.pallas_call(
        functools.partial(norm_kernel, rows, width, heads),
        out_shape=[
            jax.ShapeDtypeStruct((rows * width, channels), low),
            jax.ShapeDtypeStruct((FIRST * rows * heads, width), low),
        ],
        in_specs=in_vmem(4),
        out_specs=in_vmem(2),
        scratch_shapes=[pltpu.VMEM((rows * heads, width), wide)],
        compiler_params=params,
        name="norm",
    )(pair.reshape(rows * width, channels), ln_gain.reshape(1, channels), ln_offset.reshape(1, channels), bias_weight.T)
    *sends, present, packed = pl.pallas_call(
        functools.partial(layout_kernel, rows, width, groups, CHUNKS),
        out_shape=[jax.ShapeDtypeStruct((block, channels), low)] * CHUNKS
        + [jax.ShapeDtypeStruct((width, cols), low), jax.ShapeDtypeStruct((channels, 4 * channels), low)],
        in_specs=in_vmem(6),
        out_specs=in_vmem(CHUNKS + 2),
        scratch_shapes=[pltpu.VMEM((2, width, channels), wide)] + [pltpu.VMEM((block, channels), wide)] * CHUNKS,
        compiler_params=params,
        cost_estimate=pl.CostEstimate(flops=10**6, bytes_accessed=15 * 10**6, transcendentals=0),
        name="layout",
    )(normed, pair_mask.T, query_weight, key_weight, value_weight, gate_weight)

    pieces, sends = gather_bias(bias_copies, sends)
    whole = pl.BlockSpec(memory_space=pl.ANY)
    later = sends[1:]
    turned, *later = pl.pallas_call(
        functools.partial(turn_kernel, heads, rows, len(later)),
        out_shape=[jax.ShapeDtypeStruct((heads, width, width), low)]
        + [jax.ShapeDtypeStruct(one.shape, one.dtype) for one in later],
        in_specs=in_vmem(len(pieces)) + [whole] * len(later),
        out_specs=in_vmem(1) + [whole] * len(later),
        input_output_aliases={len(pieces) + at: 1 + at for at in range(len(later))},
        scratch_shapes=[pltpu.VMEM((width // channels, width * heads, channels), wide)],
        compiler_params=pltpu.CompilerParams(vmem_limit_bytes=TURN_MIB * 1024 * 1024),
        name="turn",
    )(*pieces, *later)
    moved = [
        lax.all_to_all(
            send.reshape(groups, rows * per, channels), "dap", split_axis=0, concat_axis=0, tiled=True
        ).reshape(block, channels)
        for send in (sends[0], *later)
    ]

    returned = []
    for chunk in range(CHUNKS):
        gated = pl.pallas_call(
            functools.partial(attend_kernel, chunk, per, heads),
            out_shape=jax.ShapeDtypeStruct((block, channels), low),
            in_specs=in_vmem(5),
            out_specs=in_vmem(1)[0],
            scratch_shapes=[
                pltpu.VMEM((block, channels), wide),
                pltpu.VMEM((block, channels), wide),
                pltpu.VMEM((8, channels), wide),
            ]
            + 2
            * [
                pltpu.VMEM((width, channels), low),
                pltpu.VMEM((width, channels), low),
                pltpu.VMEM((width, 2 * channels), low),
                pltpu.VMEM((width, channels), low),
                pltpu.VMEM((width, 2 * channels), wide),
            ],
            compiler_params=pltpu.CompilerParams(vmem_limit_bytes=ATTEND_MIB * 1024 * 1024),
            cost_estimate=pl.CostEstimate(
                flops=per * heads * width * width * channels * 6,
                bytes_accessed=2 * heads * width * width,
                transcendentals=per * heads * width * width,
            ),
            name="attend",
        )(
            moved[chunk],
            turned,
            present,
            packed,
            gate_offset.reshape(1, channels),
        )
        returned.append(
            lax.all_to_all(
                gated.reshape(groups, rows * per, channels), "dap", split_axis=0, concat_axis=0, tiled=True
            ).reshape(block, channels)
        )
    update = pl.pallas_call(
        functools.partial(finish_kernel, rows, width, groups, CHUNKS),
        out_shape=jax.ShapeDtypeStruct((rows * width, channels), low),
        in_specs=in_vmem(CHUNKS + 2),
        out_specs=in_vmem(1)[0],
        scratch_shapes=[pltpu.VMEM((block, channels), wide)] * CHUNKS + [pltpu.VMEM((2, width, channels), wide)],
        compiler_params=pltpu.CompilerParams(vmem_limit_bytes=FINISH_MIB * 1024 * 1024),
        name="finish",
    )(*returned, out_weight, out_offset.reshape(1, channels))
    return update.reshape(rows, width, channels)


def solution(mesh):
    in_specs = (P(("dp", "dap"), None, None), P("dp", "dap")) + (P(),) * 10
    out_specs = P(("dp", "dap"), None, None)
    return jax.shard_map(local, mesh=mesh, in_specs=in_specs, out_specs=out_specs, check_vma=False)
```

```python
import functools

import jax
import jax.numpy as jnp
from jax import lax
from jax.experimental import pallas as pl
from jax.experimental.pallas import tpu as pltpu
from jax.sharding import PartitionSpec as P

NEG_BIG = 1000000000.0
EPSILON = 1e-05
CHUNKS = 2
ATTEND_MIB = 40
MASK_ROWS = 16
TURN_MIB = 60
FINISH_MIB = 30
TOTAL_LOW = 1e-20
TOTAL_HIGH = 1e30
NT = (((1,), (1,)), ((), ()))
PLACE = ("z", "y", "x", "core")
PLACE_SIZES = (2, 4, 4, 2)
TOTAL = 64
FIRST = 8
SHIFTS = (0, 1, 2, 3)


def dot(lhs, rhs):
    return jnp.dot(lhs, rhs, preferred_element_type=jnp.float32)


def dot_nt(lhs, rhs):
    return lax.dot_general(lhs, rhs, NT, preferred_element_type=jnp.float32)


def in_vmem(count):
    return [pl.BlockSpec(memory_space=pltpu.VMEM)] * count


def norm_kernel(rows, width, heads, pair_ref, gain_ref, offset_ref, bias_weight_ref, normed_ref, bias_ref, wide_ref):
    weight = bias_weight_ref[...]
    blank = jnp.zeros_like(weight)
    both = jnp.concatenate(
        [jnp.concatenate([weight, blank], axis=1), jnp.concatenate([blank, weight], axis=1)], axis=0
    )
    for row in range(rows):
        wide = pair_ref[pl.ds(row * width, width), :].astype(jnp.float32)
        centred = wide - jnp.mean(wide, axis=1, keepdims=True)
        spread = jnp.mean(centred * centred, axis=1, keepdims=True)
        normed = centred * lax.rsqrt(spread + EPSILON) * gain_ref[...] + offset_ref[...]
        normed_ref[pl.ds(row * width, width), :] = normed.astype(jnp.bfloat16)
        if row % 2:
            two = [normed_ref[pl.ds(at * width, width), :] for at in (row - 1, row)]
            wide_ref[pl.ds((row - 1) * heads, 2 * heads), :] = dot_nt(both, jnp.concatenate(two, axis=1))
    for copy in range(bias_ref.shape[0] // (rows * heads)):
        bias_ref[pl.ds(copy * rows * heads, rows * heads), :] = wide_ref[...].astype(jnp.bfloat16)


def layout_kernel(rows, width, groups, chunks, normed_ref, *refs):
    chunk_refs, wide_ref, staged_refs = refs[:chunks], refs[chunks], refs[chunks + 1 :]
    cols = width // groups
    per = cols // chunks
    for row in range(rows):
        wide_ref[row % 2] = normed_ref[pl.ds(row * width, width), :].astype(jnp.float32)
        for col in range(cols):
            chunk, place = divmod(col, per)
            staged_refs[chunk][pl.ds(row * per + place, groups, stride=rows * per), :] = wide_ref[
                row % 2, pl.ds(col, groups, stride=cols), :
            ]
    for chunk in range(chunks):
        chunk_refs[chunk][...] = staged_refs[chunk][...].astype(jnp.bfloat16)


def hold_kernel(*refs):
    pass


def hold(*arrays):
    whole = [pl.BlockSpec(memory_space=pl.ANY)] * len(arrays)
    return pl.pallas_call(
        hold_kernel,
        out_shape=[jax.ShapeDtypeStruct(one.shape, one.dtype) for one in arrays],
        in_specs=whole,
        out_specs=whole,
        input_output_aliases={at: at for at in range(len(arrays))},
        name="hold",
    )(*arrays)


def place_of(index):
    place = {}
    for axis, size in zip(reversed(PLACE), reversed(PLACE_SIZES)):
        place[axis] = index % size if isinstance(index, int) else lax.rem(index, size)
        index = index // size
    return place


def index_of(place):
    index = 0
    for axis, size in zip(PLACE, PLACE_SIZES):
        index = index * size + place[axis]
    return index


ORDER = (("y", "x"), ("x", "y"))


def first_groups():
    groups = {}
    for index in range(TOTAL):
        place = place_of(index)
        groups.setdefault((place["core"], place[ORDER[place["core"]][1]]), []).append(index)
    return list(groups.values())


def second_pairs(step):
    pairs = []
    for index in range(TOTAL):
        place = place_of(index)
        axis = ORDER[place["core"]][1]
        pairs.append((index, index_of({**place, axis: (place[axis] + step) % 4})))
    return pairs


def gather_bias(bias_copies, sends):
    first = lax.all_to_all(
        bias_copies.reshape((FIRST, bias_copies.shape[0] // FIRST, bias_copies.shape[1])),
        "dap",
        split_axis=0,
        concat_axis=0,
        axis_index_groups=first_groups(),
        tiled=True,
    ).reshape(bias_copies.shape)
    first, *sends = hold(first, *sends)
    pieces = [first if step == 0 else lax.ppermute(first, "dap", second_pairs(step)) for step in SHIFTS]
    other_core = [(index, index ^ 1) for index in range(TOTAL)]
    return pieces + [lax.ppermute(piece, "dap", other_core) for piece in pieces], sends


def turn_kernel(heads, rows, handed, *refs):
    count = 2 * len(SHIFTS)
    pieces, mask_ref, weight_refs = refs[:count], refs[count], refs[count + 1 : count + 5]
    held_ref, wide_ref = refs[count + 5 + handed], refs[-1]
    width = held_ref.shape[1]
    tile = wide_ref.shape[2]
    here = place_of(lax.axis_index("dap"))
    block = rows * heads

    for other in range(2):
        core = here["core"] if other == 0 else 1 - here["core"]
        last = jnp.where(core == 0, here["x"], here["y"])
        for far, step in enumerate(SHIFTS):
            second = lax.rem(last + 4 - step, 4)
            for place in range(FIRST):
                first = place % 4
                at = {
                    "z": place // 4,
                    "y": jnp.where(core == 0, first, second),
                    "x": jnp.where(core == 0, second, first),
                    "core": core,
                }
                start = pl.multiple_of(index_of(at) * block, 16)
                for lane in range(width // tile):
                    wide_ref[lane, pl.ds(start, block), :] = pieces[other * len(SHIFTS) + far][
                        pl.ds(place * block, block), lane * tile : (lane + 1) * tile
                    ].astype(jnp.float32)

    unit = (
        lax.broadcasted_iota(jnp.int32, (tile, tile), 0) == lax.broadcasted_iota(jnp.int32, (tile, tile), 1)
    ).astype(jnp.bfloat16)
    for head in range(heads):
        for at in range(0, width, tile):
            one = wide_ref[at // tile, pl.ds(head, width, stride=heads), :].astype(jnp.bfloat16)
            held_ref[pl.ds(head * width + at, tile), :] = dot_nt(unit, one).astype(jnp.bfloat16)
    packed = jnp.concatenate([ref[...] for ref in weight_refs], axis=1)
    weight_rows = packed.shape[0]
    held_ref[pl.ds(heads * width, weight_rows), :] = jnp.concatenate(
        [packed, jnp.zeros((weight_rows, width - packed.shape[1]), jnp.bfloat16)], axis=1
    )
    mask = mask_ref[...].astype(jnp.float32)
    held_ref[pl.ds(heads * width + weight_rows, MASK_ROWS), :] = jnp.concatenate(
        [mask, jnp.zeros((MASK_ROWS - mask.shape[0], width), jnp.float32)], axis=0
    ).astype(jnp.bfloat16)


def attend_kernel(
    chunk,
    per,
    heads,
    moved_ref,
    held_ref,
    gate_offset_ref,
    out_ref,
    source_ref,
    present_ref,
    result_ref,
    fine_ref,
    *sets,
):
    channels = moved_ref.shape[1]
    width, mask_cols = present_ref.shape
    head_dim = channels // heads
    source_ref[...] = moved_ref[...].astype(jnp.float32)
    present_ref[...] = (
        held_ref[pl.ds(heads * width + channels, mask_cols), :].astype(jnp.float32).T.astype(jnp.bfloat16)
    )
    lane_head = lax.broadcasted_iota(jnp.int32, (1, channels), 1) // head_dim
    own = [(lane_head == head).astype(jnp.bfloat16) for head in range(heads)]
    fine_ref[...] = jnp.ones_like(fine_ref)
    share = width // heads
    first_set, second_set = sets[:5], sets[5:]

    def project(col, part, buffers, hide=True):
        query_ref, key_ref, value_ref, gate_ref, _ = buffers
        rows = pl.ds(part * share, share)
        source = source_ref[pl.ds(col + part * share * per, share, stride=per), :].astype(jnp.bfloat16)
        wide = dot(source, held_ref[pl.ds(heads * width, channels), : 4 * channels])
        query_ref[rows, :] = (wide[:, :channels] * head_dim ** (-0.5)).astype(jnp.bfloat16)
        key_ref[rows, :] = wide[:, channels : 2 * channels].astype(jnp.bfloat16)
        pick = (lax.broadcasted_iota(jnp.int32, (mask_cols, channels), 0) == chunk * per + col).astype(jnp.bfloat16)
        present = dot(present_ref[rows, :], pick).astype(jnp.bfloat16)
        values = wide[:, 2 * channels : 3 * channels].astype(jnp.bfloat16)
        value_ref[rows, :channels] = values * present if hide else values
        value_ref[rows, channels:] = present
        gate_ref[rows, :] = jax.nn.sigmoid(wide[:, 3 * channels :] + gate_offset_ref[...]).astype(jnp.bfloat16)

    def attend(head, buffers):
        query_ref, key_ref, value_ref, _, total_ref = buffers
        scores = dot_nt(query_ref[...] * own[head], key_ref[...]) + held_ref[pl.ds(head * width, width), :].astype(jnp.float32)
        total = dot(jnp.exp(scores).astype(jnp.bfloat16), value_ref[...])
        for low in (head * head_dim, channels + head * head_dim):
            total_ref[:, low : low + head_dim] = total[:, low : low + head_dim]

    def close(col, buffers):
        _, _, _, gate_ref, total_ref = buffers
        sums = total_ref[:, channels:]
        fine = jnp.where((sums > TOTAL_LOW) & (sums < TOTAL_HIGH), 1.0, 0.0)
        fine_ref[...] = jnp.minimum(fine_ref[...], jnp.min(fine.reshape(width // 8, 8, channels), axis=0))
        result_ref[pl.ds(col, width, stride=per), :] = (
            total_ref[:, :channels] / sums * gate_ref[...].astype(jnp.float32)
        )

    for part in range(heads):
        project(0, part, first_set)

    def two_columns(step, carry):
        for now, later, col in ((first_set, second_set, 2 * step), (second_set, first_set, 2 * step + 1)):
            for head in range(heads):
                attend(head, now)
                project(jnp.minimum(col + 1, per - 1), head, later)
            close(col, now)
        return carry

    lax.fori_loop(0, per // 2, two_columns, 0)

    @pl.when(jnp.min(fine_ref[...]) < 0.5)
    def _():
        tile = 128
        query_ref, key_ref, value_ref, gate_ref, total_ref = first_set

        def exact(col, carry):
            for part in range(heads):
                project(col, part, first_set, hide=False)
            first = (lax.broadcasted_iota(jnp.int32, (8, channels), 1) == 0).astype(jnp.bfloat16)
            lift = NEG_BIG * (dot_nt(first, value_ref[:, channels:])[:1] - 1.0)

            def rows_exact(step, inner):
                rows = pl.ds(pl.multiple_of(step * tile, tile), tile)
                for head in range(heads):
                    low = head * head_dim
                    scores = dot_nt(query_ref[rows, :] * own[head], key_ref[...])
                    scores = scores + held_ref[pl.ds(pl.multiple_of(head * width + step * tile, tile), tile), :].astype(jnp.float32) + lift
                    probs = jnp.exp(scores - jnp.max(scores, axis=1, keepdims=True))
                    totals = jnp.sum(probs, axis=1, keepdims=True)
                    attended = dot(probs.astype(jnp.bfloat16), value_ref[:, :channels]) / totals
                    total_ref[rows, low : low + head_dim] = attended[:, low : low + head_dim]
                return inner

            lax.fori_loop(0, width // tile, rows_exact, 0)
            result_ref[pl.ds(col, width, stride=per), :] = total_ref[:, :channels] * gate_ref[...].astype(jnp.float32)
            return carry

        lax.fori_loop(0, per, exact, 0)

    out_ref[...] = result_ref[...].astype(jnp.bfloat16)


def finish_kernel(rows, width, groups, chunks, *refs):
    chunk_refs = refs[:chunks]
    out_weight_ref, out_offset_ref, update_ref = refs[chunks : chunks + 3]
    wide_refs = refs[chunks + 3 : 2 * chunks + 3]
    row_ref = refs[2 * chunks + 3]
    cols = width // groups
    per = cols // chunks
    for chunk in range(chunks):
        wide_refs[chunk][...] = dot(chunk_refs[chunk][...], out_weight_ref[...]) + out_offset_ref[...]
    for row in range(rows):
        for col in range(cols):
            chunk, place = divmod(col, per)
            row_ref[row % 2, pl.ds(col, groups, stride=cols), :] = wide_refs[chunk][
                pl.ds(row * per + place, groups, stride=rows * per), :
            ]
        update_ref[pl.ds(row * width, width), :] = row_ref[row % 2].astype(jnp.bfloat16)


def local(
    pair,
    pair_mask,
    ln_gain,
    ln_offset,
    bias_weight,
    query_weight,
    key_weight,
    value_weight,
    gate_weight,
    gate_offset,
    out_weight,
    out_offset,
):
    rows, width, channels = pair.shape
    groups = lax.axis_size("dap")
    cols = width // groups
    per = cols // CHUNKS
    heads = bias_weight.shape[1]
    block = groups * rows * per
    low, wide = jnp.bfloat16, jnp.float32
    params = pltpu.CompilerParams(vmem_limit_bytes=60 * 1024 * 1024)
    normed, bias_copies = pl.pallas_call(
        functools.partial(norm_kernel, rows, width, heads),
        out_shape=[
            jax.ShapeDtypeStruct((rows * width, channels), low),
            jax.ShapeDtypeStruct((FIRST * rows * heads, width), low),
        ],
        in_specs=in_vmem(4),
        out_specs=in_vmem(2),
        scratch_shapes=[pltpu.VMEM((rows * heads, width), wide)],
        compiler_params=params,
        name="norm",
    )(pair.reshape(rows * width, channels), ln_gain.reshape(1, channels), ln_offset.reshape(1, channels), bias_weight.T)
    sends = pl.pallas_call(
        functools.partial(layout_kernel, rows, width, groups, CHUNKS),
        out_shape=[jax.ShapeDtypeStruct((block, channels), low)] * CHUNKS,
        in_specs=in_vmem(1),
        out_specs=in_vmem(CHUNKS),
        scratch_shapes=[pltpu.VMEM((2, width, channels), wide)] + [pltpu.VMEM((block, channels), wide)] * CHUNKS,
        compiler_params=params,
        cost_estimate=pl.CostEstimate(flops=10**6, bytes_accessed=15 * 10**6, transcendentals=0),
        name="layout",
    )(normed)

    pieces, sends = gather_bias(bias_copies, sends)
    whole = pl.BlockSpec(memory_space=pl.ANY)
    later = sends[1:]
    held, *later = pl.pallas_call(
        functools.partial(turn_kernel, heads, rows, len(later)),
        out_shape=[jax.ShapeDtypeStruct((heads * width + channels + MASK_ROWS, width), low)]
        + [jax.ShapeDtypeStruct(one.shape, one.dtype) for one in later],
        in_specs=in_vmem(len(pieces) + 5) + [whole] * len(later),
        out_specs=in_vmem(1) + [whole] * len(later),
        input_output_aliases={len(pieces) + 5 + at: 1 + at for at in range(len(later))},
        scratch_shapes=[pltpu.VMEM((width // channels, width * heads, channels), wide)],
        compiler_params=pltpu.CompilerParams(vmem_limit_bytes=TURN_MIB * 1024 * 1024),
        name="turn",
    )(*pieces, pair_mask.T, query_weight, key_weight, value_weight, gate_weight, *later)
    moved = [
        lax.all_to_all(
            send.reshape(groups, rows * per, channels), "dap", split_axis=0, concat_axis=0, tiled=True
        ).reshape(block, channels)
        for send in (sends[0], *later)
    ]

    returned = []
    for chunk in range(CHUNKS):
        gated = pl.pallas_call(
            functools.partial(attend_kernel, chunk, per, heads),
            out_shape=jax.ShapeDtypeStruct((block, channels), low),
            in_specs=in_vmem(3),
            out_specs=in_vmem(1)[0],
            scratch_shapes=[
                pltpu.VMEM((block, channels), wide),
                pltpu.VMEM((width, MASK_ROWS), low),
                pltpu.VMEM((block, channels), wide),
                pltpu.VMEM((8, channels), wide),
            ]
            + 2
            * [
                pltpu.VMEM((width, channels), low),
                pltpu.VMEM((width, channels), low),
                pltpu.VMEM((width, 2 * channels), low),
                pltpu.VMEM((width, channels), low),
                pltpu.VMEM((width, 2 * channels), wide),
            ],
            compiler_params=pltpu.CompilerParams(vmem_limit_bytes=ATTEND_MIB * 1024 * 1024),
            cost_estimate=pl.CostEstimate(
                flops=per * heads * width * width * channels * 6,
                bytes_accessed=2 * heads * width * width,
                transcendentals=per * heads * width * width,
            ),
            name="attend",
        )(
            moved[chunk],
            held,
            gate_offset.reshape(1, channels),
        )
        returned.append(
            lax.all_to_all(
                gated.reshape(groups, rows * per, channels), "dap", split_axis=0, concat_axis=0, tiled=True
            ).reshape(block, channels)
        )
    update = pl.pallas_call(
        functools.partial(finish_kernel, rows, width, groups, CHUNKS),
        out_shape=jax.ShapeDtypeStruct((rows * width, channels), low),
        in_specs=in_vmem(CHUNKS + 2),
        out_specs=in_vmem(1)[0],
        scratch_shapes=[pltpu.VMEM((block, channels), wide)] * CHUNKS + [pltpu.VMEM((2, width, channels), wide)],
        compiler_params=pltpu.CompilerParams(vmem_limit_bytes=FINISH_MIB * 1024 * 1024),
        name="finish",
    )(*returned, out_weight, out_offset.reshape(1, channels))
    return update.reshape(rows, width, channels)


def solution(mesh):
    in_specs = (P(("dp", "dap"), None, None), P("dp", "dap")) + (P(),) * 10
    out_specs = P(("dp", "dap"), None, None)
    return jax.shard_map(local, mesh=mesh, in_specs=in_specs, out_specs=out_specs, check_vma=False)
```

```python
import functools

import jax
import jax.numpy as jnp
from jax import lax
from jax.experimental import pallas as pl
from jax.experimental.pallas import tpu as pltpu
from jax.sharding import PartitionSpec as P

NEG_BIG = 1000000000.0
EPSILON = 1e-05
CHUNKS = 2
ATTEND_MIB = 40
MASK_ROWS = 16
TURN_MIB = 30
ROOM = 8
FINISH_MIB = 30
TOTAL_LOW = 1e-20
TOTAL_HIGH = 1e30
NT = (((1,), (1,)), ((), ()))
PLACE = ("z", "y", "x", "core")
PLACE_SIZES = (2, 4, 4, 2)
TOTAL = 64
FIRST = 8
SHIFTS = (0, 1, 2, 3)


def dot(lhs, rhs):
    return jnp.dot(lhs, rhs, preferred_element_type=jnp.float32)


def dot_nt(lhs, rhs):
    return lax.dot_general(lhs, rhs, NT, preferred_element_type=jnp.float32)


def in_vmem(count):
    return [pl.BlockSpec(memory_space=pltpu.VMEM)] * count


def normalise(block, gain_ref, offset_ref):
    wide = block.astype(jnp.float32)
    centred = wide - jnp.mean(wide, axis=1, keepdims=True)
    spread = jnp.mean(centred * centred, axis=1, keepdims=True)
    return (centred * lax.rsqrt(spread + EPSILON) * gain_ref[...] + offset_ref[...]).astype(jnp.bfloat16)


def norm_kernel(rows, width, heads, pair_ref, gain_ref, offset_ref, bias_weight_ref, bias_ref, wide_ref):
    weight = bias_weight_ref[...]
    blank = jnp.zeros_like(weight)
    both = jnp.concatenate(
        [jnp.concatenate([weight, blank], axis=1), jnp.concatenate([blank, weight], axis=1)], axis=0
    )
    for row in range(0, rows, 2):
        two = [normalise(pair_ref[pl.ds(at * width, width), :], gain_ref, offset_ref) for at in (row, row + 1)]
        wide_ref[pl.ds(row * heads, 2 * heads), :] = dot_nt(both, jnp.concatenate(two, axis=1))
    for copy in range(bias_ref.shape[0] // (rows * heads)):
        bias_ref[pl.ds(copy * rows * heads, rows * heads), :] = wide_ref[...].astype(jnp.bfloat16)


def layout_kernel(rows, width, groups, chunks, start, pair_ref, gain_ref, offset_ref, _, mask_ref, *refs):
    weight_refs, chunk_refs, whole_ref = refs[:4], refs[4 : 4 + chunks], refs[4 + chunks]
    tail_ref, sem, wide_ref = refs[5 + chunks : 8 + chunks]
    staged_refs = refs[8 + chunks :]
    packed = jnp.concatenate([ref[...] for ref in weight_refs], axis=1)
    weight_rows = packed.shape[0]
    tail_ref[pl.ds(0, weight_rows), :] = jnp.concatenate(
        [packed, jnp.zeros((weight_rows, width - packed.shape[1]), jnp.bfloat16)], axis=1
    )
    mask = mask_ref[...].astype(jnp.float32)
    tail_ref[pl.ds(weight_rows, MASK_ROWS), :] = jnp.concatenate(
        [mask, jnp.zeros((MASK_ROWS - mask.shape[0], width), jnp.float32)], axis=0
    ).astype(jnp.bfloat16)
    store = pltpu.make_async_copy(tail_ref, whole_ref.at[pl.ds(start, weight_rows + MASK_ROWS), :], sem)
    store.start()
    cols = width // groups
    per = cols // chunks
    for row in range(rows):
        normed = normalise(pair_ref[pl.ds(row * width, width), :], gain_ref, offset_ref)
        wide_ref[row % 2] = normed.astype(jnp.float32)
        for col in range(cols):
            chunk, place = divmod(col, per)
            staged_refs[chunk][pl.ds(row * per + place, groups, stride=rows * per), :] = wide_ref[
                row % 2, pl.ds(col, groups, stride=cols), :
            ]
    for chunk in range(chunks):
        chunk_refs[chunk][...] = staged_refs[chunk][...].astype(jnp.bfloat16)
    store.wait()


def hold_kernel(*refs):
    pass


def hold(*arrays):
    whole = [pl.BlockSpec(memory_space=pl.ANY)] * len(arrays)
    return pl.pallas_call(
        hold_kernel,
        out_shape=[jax.ShapeDtypeStruct(one.shape, one.dtype) for one in arrays],
        in_specs=whole,
        out_specs=whole,
        input_output_aliases={at: at for at in range(len(arrays))},
        name="hold",
    )(*arrays)


def place_of(index):
    place = {}
    for axis, size in zip(reversed(PLACE), reversed(PLACE_SIZES)):
        place[axis] = index % size if isinstance(index, int) else lax.rem(index, size)
        index = index // size
    return place


def index_of(place):
    index = 0
    for axis, size in zip(PLACE, PLACE_SIZES):
        index = index * size + place[axis]
    return index


ORDER = (("y", "x"), ("x", "y"))


def first_groups():
    groups = {}
    for index in range(TOTAL):
        place = place_of(index)
        groups.setdefault((place["core"], place[ORDER[place["core"]][1]]), []).append(index)
    return list(groups.values())


def second_pairs(step):
    pairs = []
    for index in range(TOTAL):
        place = place_of(index)
        axis = ORDER[place["core"]][1]
        pairs.append((index, index_of({**place, axis: (place[axis] + step) % 4})))
    return pairs


def gather_bias(bias_copies, sends):
    first = lax.all_to_all(
        bias_copies.reshape((FIRST, bias_copies.shape[0] // FIRST, bias_copies.shape[1])),
        "dap",
        split_axis=0,
        concat_axis=0,
        axis_index_groups=first_groups(),
        tiled=True,
    ).reshape(bias_copies.shape)
    first, *sends = hold(first, *sends)
    pieces = [first if step == 0 else lax.ppermute(first, "dap", second_pairs(step)) for step in SHIFTS]
    other_core = [(index, index ^ 1) for index in range(TOTAL)]
    return pieces + [lax.ppermute(piece, "dap", other_core) for piece in pieces], sends


def turn_kernel(heads, rows, handed, *refs):
    count = 2 * len(SHIFTS)
    pieces, whole_ref, (held_ref, wide_ref, sems) = refs[:count], refs[count + 1 + handed], refs[-3:]
    width = held_ref.shape[1]
    tile = wide_ref.shape[2]
    here = place_of(lax.axis_index("dap"))
    block = rows * heads

    for other in range(2):
        core = here["core"] if other == 0 else 1 - here["core"]
        last = jnp.where(core == 0, here["x"], here["y"])
        for far, step in enumerate(SHIFTS):
            second = lax.rem(last + 4 - step, 4)
            for place in range(FIRST):
                first = place % 4
                at = {
                    "z": place // 4,
                    "y": jnp.where(core == 0, first, second),
                    "x": jnp.where(core == 0, second, first),
                    "core": core,
                }
                start = pl.multiple_of(index_of(at) * block, 16)
                for lane in range(width // tile):
                    wide_ref[lane, pl.ds(start, block), :] = pieces[other * len(SHIFTS) + far][
                        pl.ds(place * block, block), lane * tile : (lane + 1) * tile
                    ].astype(jnp.float32)

    unit = (
        lax.broadcasted_iota(jnp.int32, (tile, tile), 0) == lax.broadcasted_iota(jnp.int32, (tile, tile), 1)
    ).astype(jnp.bfloat16)
    stores = []

    def store(at, rows_of):
        stores.append(pltpu.make_async_copy(held_ref.at[rows_of, :], whole_ref.at[rows_of, :], sems.at[at]))
        stores[at].start()

    for head in range(heads):
        for at in range(0, width, tile):
            one = wide_ref[at // tile, pl.ds(head, width, stride=heads), :].astype(jnp.bfloat16)
            held_ref[pl.ds(head * width + at, tile), :] = dot_nt(unit, one).astype(jnp.bfloat16)
        store(head, pl.ds(head * width, width))
    for one in stores:
        one.wait()


def attend_kernel(
    chunk,
    per,
    heads,
    moved_ref,
    held_ref,
    gate_offset_ref,
    out_ref,
    source_ref,
    present_ref,
    result_ref,
    fine_ref,
    *sets,
):
    channels = moved_ref.shape[1]
    width, mask_cols = present_ref.shape
    head_dim = channels // heads
    source_ref[...] = moved_ref[...].astype(jnp.float32)
    present_ref[...] = (
        held_ref[pl.ds(heads * width + channels, mask_cols), :].astype(jnp.float32).T.astype(jnp.bfloat16)
    )
    lane_head = lax.broadcasted_iota(jnp.int32, (1, channels), 1) // head_dim
    own = [(lane_head == head).astype(jnp.bfloat16) for head in range(heads)]
    fine_ref[...] = jnp.ones_like(fine_ref)
    share = width // heads
    first_set, second_set = sets[:5], sets[5:]

    def project(col, part, buffers, hide=True):
        query_ref, key_ref, value_ref, gate_ref, _ = buffers
        rows = pl.ds(part * share, share)
        source = source_ref[pl.ds(col + part * share * per, share, stride=per), :].astype(jnp.bfloat16)
        wide = dot(source, held_ref[pl.ds(heads * width, channels), : 4 * channels])
        query_ref[rows, :] = (wide[:, :channels] * head_dim ** (-0.5)).astype(jnp.bfloat16)
        key_ref[rows, :] = wide[:, channels : 2 * channels].astype(jnp.bfloat16)
        pick = (lax.broadcasted_iota(jnp.int32, (mask_cols, channels), 0) == chunk * per + col).astype(jnp.bfloat16)
        present = dot(present_ref[rows, :], pick).astype(jnp.bfloat16)
        values = wide[:, 2 * channels : 3 * channels].astype(jnp.bfloat16)
        value_ref[rows, :channels] = values * present if hide else values
        value_ref[rows, channels:] = present
        gate_ref[rows, :] = jax.nn.sigmoid(wide[:, 3 * channels :] + gate_offset_ref[...]).astype(jnp.bfloat16)

    def attend(head, buffers):
        query_ref, key_ref, value_ref, _, total_ref = buffers
        scores = dot_nt(query_ref[...] * own[head], key_ref[...]) + held_ref[pl.ds(head * width, width), :].astype(jnp.float32)
        total = dot(jnp.exp(scores).astype(jnp.bfloat16), value_ref[...])
        for low in (head * head_dim, channels + head * head_dim):
            total_ref[:, low : low + head_dim] = total[:, low : low + head_dim]

    def close(col, buffers):
        _, _, _, gate_ref, total_ref = buffers
        sums = total_ref[:, channels:]
        fine = jnp.where((sums > TOTAL_LOW) & (sums < TOTAL_HIGH), 1.0, 0.0)
        fine_ref[...] = jnp.minimum(fine_ref[...], jnp.min(fine.reshape(width // 8, 8, channels), axis=0))
        result_ref[pl.ds(col, width, stride=per), :] = (
            total_ref[:, :channels] / sums * gate_ref[...].astype(jnp.float32)
        )

    for part in range(heads):
        project(0, part, first_set)

    def two_columns(step, carry):
        for now, later, col in ((first_set, second_set, 2 * step), (second_set, first_set, 2 * step + 1)):
            for head in range(heads):
                attend(head, now)
                project(jnp.minimum(col + 1, per - 1), head, later)
            close(col, now)
        return carry

    lax.fori_loop(0, per // 2, two_columns, 0)

    @pl.when(jnp.min(fine_ref[...]) < 0.5)
    def _():
        tile = 128
        query_ref, key_ref, value_ref, gate_ref, total_ref = first_set

        def exact(col, carry):
            for part in range(heads):
                project(col, part, first_set, hide=False)
            first = (lax.broadcasted_iota(jnp.int32, (8, channels), 1) == 0).astype(jnp.bfloat16)
            lift = NEG_BIG * (dot_nt(first, value_ref[:, channels:])[:1] - 1.0)

            def rows_exact(step, inner):
                rows = pl.ds(pl.multiple_of(step * tile, tile), tile)
                for head in range(heads):
                    low = head * head_dim
                    scores = dot_nt(query_ref[rows, :] * own[head], key_ref[...])
                    scores = scores + held_ref[pl.ds(pl.multiple_of(head * width + step * tile, tile), tile), :].astype(jnp.float32) + lift
                    probs = jnp.exp(scores - jnp.max(scores, axis=1, keepdims=True))
                    totals = jnp.sum(probs, axis=1, keepdims=True)
                    attended = dot(probs.astype(jnp.bfloat16), value_ref[:, :channels]) / totals
                    total_ref[rows, low : low + head_dim] = attended[:, low : low + head_dim]
                return inner

            lax.fori_loop(0, width // tile, rows_exact, 0)
            result_ref[pl.ds(col, width, stride=per), :] = total_ref[:, :channels] * gate_ref[...].astype(jnp.float32)
            return carry

        lax.fori_loop(0, per, exact, 0)

    out_ref[...] = result_ref[...].astype(jnp.bfloat16)


def finish_kernel(rows, width, groups, chunks, *refs):
    chunk_refs = refs[:chunks]
    out_weight_ref, out_offset_ref, update_ref = refs[chunks : chunks + 3]
    wide_refs = refs[chunks + 3 : 2 * chunks + 3]
    row_ref = refs[2 * chunks + 3]
    cols = width // groups
    per = cols // chunks
    for chunk in range(chunks):
        wide_refs[chunk][...] = dot(chunk_refs[chunk][...], out_weight_ref[...]) + out_offset_ref[...]
    for row in range(rows):
        for col in range(cols):
            chunk, place = divmod(col, per)
            row_ref[row % 2, pl.ds(col, groups, stride=cols), :] = wide_refs[chunk][
                pl.ds(row * per + place, groups, stride=rows * per), :
            ]
        update_ref[pl.ds(row * width, width), :] = row_ref[row % 2].astype(jnp.bfloat16)


def local(
    pair,
    pair_mask,
    ln_gain,
    ln_offset,
    bias_weight,
    query_weight,
    key_weight,
    value_weight,
    gate_weight,
    gate_offset,
    out_weight,
    out_offset,
):
    rows, width, channels = pair.shape
    groups = lax.axis_size("dap")
    cols = width // groups
    per = cols // CHUNKS
    heads = bias_weight.shape[1]
    block = groups * rows * per
    low, wide = jnp.bfloat16, jnp.float32
    params = pltpu.CompilerParams(vmem_limit_bytes=60 * 1024 * 1024)
    flat = (pair.reshape(rows * width, channels), ln_gain.reshape(1, channels), ln_offset.reshape(1, channels))
    bias_copies = pl.pallas_call(
        functools.partial(norm_kernel, rows, width, heads),
        out_shape=jax.ShapeDtypeStruct((FIRST * rows * heads, width), low),
        in_specs=in_vmem(4),
        out_specs=in_vmem(1)[0],
        scratch_shapes=[pltpu.VMEM((rows * heads, width), wide)],
        compiler_params=params,
        name="norm",
    )(*flat, bias_weight.T)
    whole = pl.BlockSpec(memory_space=pl.ANY)
    tail_rows = channels + MASK_ROWS
    held_rows = heads * width + tail_rows
    *sends, held = pl.pallas_call(
        functools.partial(layout_kernel, rows, width, groups, CHUNKS, heads * width),
        out_shape=[jax.ShapeDtypeStruct((block, channels), low)] * CHUNKS
        + [jax.ShapeDtypeStruct((ROOM * held_rows, width), low)],
        in_specs=in_vmem(3) + [whole] + in_vmem(5),
        out_specs=in_vmem(CHUNKS) + [whole],
        scratch_shapes=[
            pltpu.VMEM((tail_rows, width), low),
            pltpu.SemaphoreType.DMA,
            pltpu.VMEM((2, width, channels), wide),
        ]
        + [pltpu.VMEM((block, channels), wide)] * CHUNKS,
        compiler_params=params,
        cost_estimate=pl.CostEstimate(flops=10**6, bytes_accessed=15 * 10**6, transcendentals=0),
        name="layout",
    )(*flat, bias_copies, pair_mask.T, query_weight, key_weight, value_weight, gate_weight)

    pieces, sends = gather_bias(bias_copies, sends)
    later = sends[1:]
    held, *later = pl.pallas_call(
        functools.partial(turn_kernel, heads, rows, len(later)),
        out_shape=[jax.ShapeDtypeStruct(one.shape, one.dtype) for one in (held, *later)],
        in_specs=in_vmem(len(pieces)) + [whole] * (1 + len(later)),
        out_specs=[whole] * (1 + len(later)),
        input_output_aliases={len(pieces) + at: at for at in range(1 + len(later))},
        scratch_shapes=[
            pltpu.VMEM((heads * width, width), low),
            pltpu.VMEM((width // channels, width * heads, channels), wide),
            pltpu.SemaphoreType.DMA((heads,)),
        ],
        compiler_params=pltpu.CompilerParams(vmem_limit_bytes=TURN_MIB * 1024 * 1024),
        name="turn",
    )(*pieces, held, *later)
    moved = [
        lax.all_to_all(
            send.reshape(groups, rows * per, channels), "dap", split_axis=0, concat_axis=0, tiled=True
        ).reshape(block, channels)
        for send in (sends[0], *later)
    ]

    returned = []
    for chunk in range(CHUNKS):
        gated = pl.pallas_call(
            functools.partial(attend_kernel, chunk, per, heads),
            out_shape=jax.ShapeDtypeStruct((block, channels), low),
            grid=(1,),
            in_specs=in_vmem(1)
            + [pl.BlockSpec((held_rows, width), lambda step: (0, 0), pipeline_mode=pl.Buffered(1))]
            + in_vmem(1),
            out_specs=in_vmem(1)[0],
            scratch_shapes=[
                pltpu.VMEM((block, channels), wide),
                pltpu.VMEM((width, MASK_ROWS), low),
                pltpu.VMEM((block, channels), wide),
                pltpu.VMEM((8, channels), wide),
            ]
            + 2
            * [
                pltpu.VMEM((width, channels), low),
                pltpu.VMEM((width, channels), low),
                pltpu.VMEM((width, 2 * channels), low),
                pltpu.VMEM((width, channels), low),
                pltpu.VMEM((width, 2 * channels), wide),
            ],
            compiler_params=pltpu.CompilerParams(vmem_limit_bytes=ATTEND_MIB * 1024 * 1024),
            cost_estimate=pl.CostEstimate(
                flops=per * heads * width * width * channels * 6,
                bytes_accessed=2 * heads * width * width,
                transcendentals=per * heads * width * width,
            ),
            name="attend",
        )(
            moved[chunk],
            held,
            gate_offset.reshape(1, channels),
        )
        returned.append(
            lax.all_to_all(
                gated.reshape(groups, rows * per, channels), "dap", split_axis=0, concat_axis=0, tiled=True
            ).reshape(block, channels)
        )
    update = pl.pallas_call(
        functools.partial(finish_kernel, rows, width, groups, CHUNKS),
        out_shape=jax.ShapeDtypeStruct((rows * width, channels), low),
        in_specs=in_vmem(CHUNKS + 2),
        out_specs=in_vmem(1)[0],
        scratch_shapes=[pltpu.VMEM((block, channels), wide)] * CHUNKS + [pltpu.VMEM((2, width, channels), wide)],
        compiler_params=pltpu.CompilerParams(vmem_limit_bytes=FINISH_MIB * 1024 * 1024),
        name="finish",
    )(*returned, out_weight, out_offset.reshape(1, channels))
    return update.reshape(rows, width, channels)


def solution(mesh):
    in_specs = (P(("dp", "dap"), None, None), P("dp", "dap")) + (P(),) * 10
    out_specs = P(("dp", "dap"), None, None)
    return jax.shard_map(local, mesh=mesh, in_specs=in_specs, out_specs=out_specs, check_vma=False)
```
